32 devices in a mesh: slab: 8 (over y, x, core), sub: 4 (over z).
Axes of the slice: x: 2, y: 2, z: 4, core: 2. Of those that a mesh axis runs over, the one named last changes fastest.
Arguments:
- field_init: float32 [3, 64, 64, 128], P(None, 'slab', 'sub'), may hold values from -6 to 6
- load: float32 [3, 64, 64, 128], P(None, 'slab', 'sub'), may hold values from -6 to 6
- modulus: float32 [64, 64, 128], P('slab', 'sub'), may hold values from 0.3 to 3
- seg_z: int32 [64], P('slab'), may hold values from 0 to 15, as said below
- seg_y: int32 [64], P('sub'), may hold values from 0 to 15, as said below
- seg_x: int32 [128], replicated, may hold values from 0 to 31, as said below
Outputs:
- smoothed: float32 [3, 64, 64, 128], P(None, 'slab', 'sub')
- coarse: float32 [6, 16, 512], P(None, 'slab', 'sub')
The draws below stay inside these ranges and needn't reach their ends.
Inputs may be any that keep to these rules, and one draw needn't show every extreme that they name: `seg_z`: along z, segment k starts at node 4 k or 4 k + 1 (segment 0 at 0, the last segment at 4 k + 1) and runs to the next start or the grid's end; entries never fall. `seg_y`: along y, segment k starts at node 4 k or 4 k + 1 (segment 0 at 0, the last segment at 4 k + 1) and runs to the next start or the grid's end; entries never fall. `seg_x`: along x, segment k starts at node 4 k or 4 k + 1 (segment 0 at 0, the last segment at 4 k + 1) and runs to the next start or the grid's end; entries never fall.
All inputs are finite; a program needn't handle non-finite values.
Results may differ from the reference program's by a relative error of at most 0.0003.
Values sent between devices are 32-bit elements; how exact they have to be, the bound alone decides.
A program may use at most 64 MiB of HBM per device.

```python
import math
import jax
import jax.numpy as jnp
import numpy as np
from jax import lax

CX = 128
CZ = 8
SWEEPS = 2
SX = 32
NY = 64
NZ = 64
NSY = 16
NSZ = 16
N_SLAB = 8


def segment_index(key, extent, pieces):
    jitter = jax.random.randint(key, (pieces,), 0, 2).astype(jnp.int32)
    order = jnp.arange(pieces, dtype=jnp.int32)
    jitter = jitter * (order > 0).astype(jnp.int32)
    jitter = jnp.where(order == pieces - 1, jnp.int32(1), jitter).astype(jnp.int32)
    starts = 4 * order + jitter
    places = jnp.arange(extent, dtype=jnp.int32)
    return (jnp.sum((places[:, None] >= starts[None, :]).astype(jnp.int32), axis=1) - 1).astype(jnp.int32)


def draw_seg_z(key, part):
    return segment_index(jax.random.fold_in(key, 11), NZ, NSZ)


def draw_seg_y(key, part):
    return segment_index(jax.random.fold_in(key, 23), NY, NSY)


def draw_seg_x(key, part):
    return segment_index(jax.random.fold_in(key, 37), CX, SX)


def block_levels(stream_key, dims, cuts, smallest, largest):
    def one(axis_at, blocks):
        draws = jax.random.uniform(jax.random.fold_in(jax.random.fold_in(stream_key, 6), axis_at), (blocks,), jnp.float32, smallest / len(cuts), largest / len(cuts))
        return jnp.repeat(jnp.exp(draws), dims[axis_at] // blocks).reshape((-1,) + (1,) * (len(dims) - axis_at - 1))

    factor_of = one(*cuts[0])
    for cut in cuts[1:]:
        factor_of = factor_of * one(*cut)
    return factor_of


def normal_values(key, shape, width, limit, cuts=(), kind=jnp.bfloat16):
    values = jax.random.normal(key, shape, jnp.float32) * width
    if len(cuts) > 0:
        values = block_levels(key, shape, cuts, -0.22, 0.18) * values
    return jnp.clip(values, min=-limit, max=limit).astype(kind)


def setup_inputs(seed: int = 0) -> dict:
    arg_keys = jax.random.split(jax.random.key(seed), 7)
    field_init = normal_values(arg_keys[0], (3, NZ, NY, CX), 1.0, 6.0, ((1, 8), (2, 4)), jnp.float32)
    load = normal_values(arg_keys[1], (3, NZ, NY, CX), 1.0, 6.0, ((1, 8), (2, 4)), jnp.float32)
    modulus = jnp.clip(jnp.exp(math.log(3.0) - 2.3025851 * jax.random.uniform(arg_keys[2], (NZ, NY, CX), jnp.float32) ** block_levels(arg_keys[2], (NZ, NY, CX), ((0, 8), (1, 4)), -0.2, 0.2)), 0.3, 3.0)
    seg_z = draw_seg_z(jax.random.fold_in(arg_keys[6], 71), 0)
    seg_y = draw_seg_y(jax.random.fold_in(arg_keys[6], 71), 0)
    seg_x = draw_seg_x(jax.random.fold_in(arg_keys[6], 71), 0)
    return dict(field_init=field_init, load=load, modulus=modulus, seg_z=seg_z, seg_y=seg_y, seg_x=seg_x)


damping = 0.6

def hex_stiffness():
    poisson = 0.3
    lame_first = poisson / ((1.0 + poisson) * (1.0 - 2.0 * poisson))
    lame_shear = 0.5 / (1.0 + poisson)
    elastic = np.zeros((6, 6))
    elastic[:3, :3] = lame_first
    for entry in range(3):
        elastic[entry, entry] += 2.0 * lame_shear
        elastic[entry + 3, entry + 3] = lame_shear
    points = [0.5 - 0.5 / np.sqrt(3.0), 0.5 + 0.5 / np.sqrt(3.0)]
    stiffness = np.zeros((24, 24))
    for point_z in points:
        for point_y in points:
            for point_x in points:
                strain = np.zeros((6, 24))
                for corner in range(8):
                    corner_z, corner_y, corner_x = (corner // 4, corner // 2 % 2, corner % 2)
                    shape_x = point_x if corner_x else 1.0 - point_x
                    shape_y = point_y if corner_y else 1.0 - point_y
                    shape_z = point_z if corner_z else 1.0 - point_z
                    slope_x = (1.0 if corner_x else -1.0) * shape_y * shape_z
                    slope_y = (1.0 if corner_y else -1.0) * shape_x * shape_z
                    slope_z = (1.0 if corner_z else -1.0) * shape_x * shape_y
                    column = 3 * corner
                    strain[0, column] = slope_x
                    strain[1, column + 1] = slope_y
                    strain[2, column + 2] = slope_z
                    strain[3, column] = slope_y
                    strain[3, column + 1] = slope_x
                    strain[4, column + 1] = slope_z
                    strain[4, column + 2] = slope_y
                    strain[5, column] = slope_z
                    strain[5, column + 2] = slope_x
                stiffness += strain.T @ elastic @ strain / 8.0
    return stiffness

def shift_right(values):
    return jnp.concatenate([jnp.zeros_like(values[..., :1]), values[..., :-1]], axis=-1)

def shift_left(values):
    return jnp.concatenate([values[..., 1:], jnp.zeros_like(values[..., :1])], axis=-1)

def apply_op(field_ext, mod_ext, table):
    depth = field_ext.shape[1] - 2
    rows = field_ext.shape[2] - 2
    element = mod_ext[:depth + 1, :rows + 1, :]
    corners = []
    for corner in range(8):
        corner_z, corner_y, corner_x = (corner // 4, corner // 2 % 2, corner % 2)
        piece = field_ext[:, corner_z:corner_z + depth + 1, corner_y:corner_y + rows + 1, :]
        if corner_x:
            piece = shift_left(piece)
        corners.append(piece)
    stacked = jnp.concatenate(corners, axis=0)
    forces = jnp.einsum('ij,jzyx->izyx', table, stacked, precision=lax.Precision.HIGHEST) * element[None]
    result = jnp.zeros((3, depth, rows, field_ext.shape[3]), jnp.float32)
    for corner in range(8):
        corner_z, corner_y, corner_x = (corner // 4, corner // 2 % 2, corner % 2)
        piece = forces[3 * corner:3 * corner + 3, 1 - corner_z:1 - corner_z + depth, 1 - corner_y:1 - corner_y + rows, :]
        if corner_x:
            piece = shift_right(piece)
        result = result + piece
    return result

def inverse_blocks(mod_ext, outside, table):
    depth = mod_ext.shape[0] - 2
    rows = mod_ext.shape[1] - 2
    diagonal = jnp.zeros((3, 3, depth, rows, mod_ext.shape[2]), jnp.float32)
    for corner in range(8):
        corner_z, corner_y, corner_x = (corner // 4, corner // 2 % 2, corner % 2)
        piece = mod_ext[1 - corner_z:1 - corner_z + depth, 1 - corner_y:1 - corner_y + rows, :]
        if corner_x:
            piece = shift_right(piece)
        block = table[3 * corner:3 * corner + 3, 3 * corner:3 * corner + 3]
        diagonal = diagonal + block[:, :, None, None, None] * piece[None, None]
    diagonal = diagonal + jnp.eye(3, dtype=jnp.float32)[:, :, None, None, None] * outside[None, None]
    a00, a01, a02 = (diagonal[0, 0], diagonal[0, 1], diagonal[0, 2])
    a10, a11, a12 = (diagonal[1, 0], diagonal[1, 1], diagonal[1, 2])
    a20, a21, a22 = (diagonal[2, 0], diagonal[2, 1], diagonal[2, 2])
    co00 = a11 * a22 - a12 * a21
    co01 = a12 * a20 - a10 * a22
    co02 = a10 * a21 - a11 * a20
    determinant = a00 * co00 + a01 * co01 + a02 * co02
    rows_inv = [[co00, a02 * a21 - a01 * a22, a01 * a12 - a02 * a11], [co01, a00 * a22 - a02 * a20, a02 * a10 - a00 * a12], [co02, a01 * a20 - a00 * a21, a00 * a11 - a01 * a10]]
    return jnp.stack([jnp.stack(line, axis=0) for line in rows_inv], axis=0) / determinant[None, None]

def block_mult(inverse, vector):
    return lax.optimization_barrier(jnp.sum(inverse * vector[None], axis=1))

def cross(first, second):
    return (first[1] * second[2] - first[2] * second[1], first[2] * second[0] - first[0] * second[2], first[0] * second[1] - first[1] * second[0])

def node_terms(residual, offset_x, offset_y, offset_z):
    shape = residual.shape[1:]
    offsets = [jnp.broadcast_to(offset_x, shape), jnp.broadcast_to(offset_y, shape), jnp.broadcast_to(offset_z, shape)]
    turned = cross(offsets, [residual[0], residual[1], residual[2]])
    return [residual[0], residual[1], residual[2], turned[0], turned[1], turned[2], offsets[0], offsets[1], offsets[2], jnp.ones(shape, jnp.float32)]

def finalize(sums):
    count = sums[9]
    norm_root = jnp.sqrt(count)
    centre = [sums[6] / count, sums[7] / count, sums[8] / count]
    moved = [sums[0], sums[1], sums[2]]
    turned = cross(centre, moved)
    rotation = [sums[3 + k] - turned[k] for k in range(3)]
    return jnp.stack(moved + rotation, axis=0) / norm_root[None]

def reference(field_init, load, modulus, seg_z, seg_y, seg_x):
    table = jnp.asarray(hex_stiffness(), jnp.float32)
    total_z, total_y, width_x = modulus.shape
    keep = (jnp.arange(total_z) < total_z - 1)[:, None, None] & (jnp.arange(total_y) < total_y - 1)[None, :, None] & (jnp.arange(width_x) < width_x - 1)[None, None, :]
    masked = jnp.where(keep, modulus, jnp.float32(0.0))
    mod_pad = jnp.pad(masked, ((1, 1), (1, 1), (0, 0)))
    no_outside = jnp.zeros((CZ, total_y, width_x), jnp.float32)
    zero_index = jnp.int32(0)

    def pass_blocks(field, update):
        field_pad = jnp.pad(field, ((0, 0), (1, 1), (1, 1), (0, 0)))

        def one_block(index):
            anchor = (index * CZ).astype(jnp.int32)
            field_blk = lax.dynamic_slice(field_pad, (zero_index, anchor, zero_index, zero_index), (3, CZ + 2, total_y + 2, width_x))
            mod_blk = lax.dynamic_slice(mod_pad, (anchor, zero_index, zero_index), (CZ + 2, total_y + 2, width_x))
            load_blk = lax.dynamic_slice(load, (zero_index, anchor, zero_index, zero_index), (3, CZ, total_y, width_x))
            misfit = load_blk - apply_op(field_blk, mod_blk, table)
            if update:
                inverse = inverse_blocks(mod_blk, no_outside, table)
                return field_blk[:, 1:-1, 1:-1, :] + damping * block_mult(inverse, misfit)
            return misfit
        blocks = lax.map(one_block, jnp.arange(N_SLAB, dtype=jnp.int32))
        return jnp.moveaxis(blocks, 0, 1).reshape(3, total_z, total_y, width_x)
    field = field_init
    for sweep in range(SWEEPS):
        field = pass_blocks(field, True)
    residual = pass_blocks(field, False)
    seg_xx = seg_x.astype(jnp.int32)[None, None, :]
    seg_yy = seg_y.astype(jnp.int32)[None, :, None]
    seg_zz = seg_z.astype(jnp.int32)[:, None, None]
    place_x = jnp.arange(width_x, dtype=jnp.int32)[None, None, :]
    place_y = jnp.arange(total_y, dtype=jnp.int32)[None, :, None]
    place_z = jnp.arange(total_z, dtype=jnp.int32)[:, None, None]
    offset_x = 0.5 * (place_x - 4 * seg_xx - 2).astype(jnp.float32)
    offset_y = 0.5 * (place_y - 4 * seg_yy - 2).astype(jnp.float32)
    offset_z = 0.5 * (place_z - 4 * seg_zz - 2).astype(jnp.float32)
    terms = node_terms(residual, offset_x, offset_y, offset_z)
    ids = ((seg_zz * NSY + seg_yy) * SX + seg_xx).astype(jnp.int32)
    flat_ids = jnp.broadcast_to(ids, (total_z, total_y, width_x)).reshape(-1)
    sums = jnp.stack([jax.ops.segment_sum(term.reshape(-1), flat_ids, num_segments=NSZ * NSY * SX) for term in terms], axis=0)
    coarse = finalize(sums.reshape(10, NSZ, NSY, SX)).reshape(6, NSZ, NSY * SX)
    return (field, coarse)
```

```python
import functools

import jax
import jax.numpy as jnp
from jax import lax
from jax.experimental import pallas as pl
from jax.experimental.pallas import tpu as pltpu
from jax.sharding import PartitionSpec as P

SWEEPS = 2
DAMPING = 0.6
LOW = SWEEPS + 1
HIGH = SWEEPS + 2
REACH = ((LOW, HIGH), (LOW - 1, HIGH - 1), (LOW, HIGH - 1))
POISSON = 0.3
LAME = POISSON / ((1.0 + POISSON) * (1.0 - 2.0 * POISSON))
SHEAR = 0.5 / (1.0 + POISSON)
SIDES = [(dz, dy) for dz in (-1, 1, 0) for dy in (0, -1, 1) if (dz, dy) != (0, 0)]
MESH = pl.DeviceIdType.MESH
F32 = jnp.float32


def spans(step, size, reach):
    low, high = reach
    if step == 1:
        return (size - low, LOW - low, low)
    if step == -1:
        return (0, LOW + size, high)
    return (0, LOW, size)


def halo_kernel(field, load, mod, seg_z, seg_y, ext, mark, send_sem, recv_sem, own_sem):
    size_z, size_y = mod.shape[0], mod.shape[1]
    slab, sub = lax.axis_index("slab"), lax.axis_index("sub")
    slabs, subs = lax.axis_size("slab"), lax.axis_size("sub")

    def present(dz, dy):
        there = jnp.bool_(True)
        if dz == 1:
            there = there & (slab < slabs - 1)
        if dz == -1:
            there = there & (slab > 0)
        if dy == 1:
            there = there & (sub < subs - 1)
        if dy == -1:
            there = there & (sub > 0)
        return there

    barrier = pltpu.get_barrier_semaphore()
    for dz, dy in SIDES:

        @pl.when(present(dz, dy))
        def _():
            pl.semaphore_signal(
                barrier, inc=1, device_id=(slab + dz, sub + dy), device_id_type=MESH
            )

    own = [
        pltpu.make_async_copy(
            src, ext.at[pl.ds(3 * k, 3), pl.ds(LOW, size_z), pl.ds(LOW, size_y)], own_sem.at[k]
        )
        for k, src in enumerate((field, load))
    ]
    own.append(
        pltpu.make_async_copy(
            mod, ext.at[6, pl.ds(LOW, size_z), pl.ds(LOW, size_y)], own_sem.at[2]
        )
    )
    for copy in own:
        copy.start()
    mark[0] = jnp.full((1, mark.shape[-1]), seg_z[0].astype(F32))
    mark[1] = jnp.full((1, mark.shape[-1]), seg_y[0].astype(F32))
    peers_z = 3 - (slab == 0).astype(jnp.int32) - (slab == slabs - 1).astype(jnp.int32)
    peers_y = 3 - (sub == 0).astype(jnp.int32) - (sub == subs - 1).astype(jnp.int32)
    pl.semaphore_wait(barrier, peers_z * peers_y - 1)

    copies = []
    for side, (dz, dy) in enumerate(SIDES):
        there = (slab + dz, sub + dy)
        group = []
        for k, src in enumerate((field, load, mod)):
            sz, tz, nz = spans(dz, size_z, REACH[k])
            sy, ty, ny = spans(dy, size_y, REACH[k])
            if k < 2:
                from_ref = src.at[:, pl.ds(sz, nz), pl.ds(sy, ny)]
                to_ref = ext.at[pl.ds(3 * k, 3), pl.ds(tz, nz), pl.ds(ty, ny)]
            else:
                from_ref = src.at[pl.ds(sz, nz), pl.ds(sy, ny)]
                to_ref = ext.at[6, pl.ds(tz, nz), pl.ds(ty, ny)]
            group.append((from_ref, to_ref, k))
        if (dz, dy) == (-1, 0):
            group.append((mark.at[0], ext.at[6, ext.shape[1] - 1, 0], 3))
        if (dz, dy) == (0, -1):
            group.append((mark.at[1], ext.at[6, ext.shape[1] - 1, 1], 3))
        group = [
            pltpu.make_async_remote_copy(
                src_ref=from_ref,
                dst_ref=to_ref,
                send_sem=send_sem.at[side, k],
                recv_sem=recv_sem.at[side, k],
                device_id=there,
                device_id_type=MESH,
            )
            for from_ref, to_ref, k in group
        ]
        copies.append(group)

        @pl.when(present(dz, dy))
        def _():
            for copy in group:
                copy.start()

    for copy in own:
        copy.wait()
    for (dz, dy), group in zip(SIDES, copies):

        @pl.when(present(dz, dy))
        def _():
            for copy in group:
                copy.wait_send()

        @pl.when(present(-dz, -dy))
        def _():
            for copy in group:
                copy.wait_recv()


def element_modes(lo, hi, e):
    def up(c, x, y):
        return lo[c][x][y] + hi[c][x][y]

    def diff(c, x, y):
        return hi[c][x][y] - lo[c][x][y]

    e_shear = e * (SHEAR / 16.0)
    e_shear2 = e * (SHEAR / 8.0)
    e_lame = e * (LAME / 16.0)
    e_lame3 = e * (LAME / 48.0)
    e_shear3 = e * (SHEAR / 48.0)
    e_last = e * ((LAME + 4.0 * SHEAR) / 144.0)
    out = [[[[None, None], [None, None]] for _ in range(2)] for _ in range(3)]

    n0, n1, n2 = up(0, 1, 0), up(1, 0, 1), diff(2, 0, 0)
    both = e_lame * (n0 + n1 + n2)
    out[0][1][0][0] = both + e_shear2 * n0
    out[1][0][1][0] = both + e_shear2 * n1
    out[2][0][0][1] = both + e_shear2 * n2

    both = e_shear * (up(0, 0, 1) + up(1, 1, 0))
    out[0][0][1][0] = both
    out[1][1][0][0] = both
    both = e_shear * (diff(0, 0, 0) + up(2, 1, 0))
    out[0][0][0][1] = both
    out[2][1][0][0] = both
    both = e_shear * (diff(1, 0, 0) + up(2, 0, 1))
    out[1][0][0][1] = both
    out[2][0][1][0] = both

    a, b = up(0, 1, 1), diff(2, 0, 1)
    both = e_lame3 * (a + b)
    out[0][1][1][0] = both + e_shear * a
    out[2][0][1][1] = both + e_shear * b
    a, b = diff(0, 1, 0), diff(1, 0, 1)
    both = e_lame3 * (a + b)
    out[0][1][0][1] = both + e_shear * a
    out[1][0][1][1] = both + e_shear * b
    a, b = up(1, 1, 1), diff(2, 1, 0)
    both = e_lame3 * (a + b)
    out[1][1][1][0] = both + e_shear * a
    out[2][1][0][1] = both + e_shear * b

    a, b, c = diff(0, 0, 1), diff(1, 1, 0), up(2, 1, 1)
    both = a + b + c
    out[0][0][1][1] = e_shear3 * (both + a)
    out[1][1][0][1] = e_shear3 * (both + b)
    out[2][1][1][0] = e_shear3 * (both + c)

    for c in range(3):
        out[c][1][1][1] = e_last * diff(c, 1, 1)
    return out


def compute_kernel(
    seg_z, seg_y, seg_x, ext, smooth, coarse, cur, emod, inverse, modes, back, resid, *, unroll
):
    size_z, size_y, width = smooth.shape[1:]
    planes, rows = ext.shape[1], ext.shape[2]
    slab, sub = lax.axis_index("slab"), lax.axis_index("sub")
    total_z = size_z * lax.axis_size("slab")
    total_y = size_y * lax.axis_size("sub")
    first_z = slab * size_z - LOW
    first_y = sub * size_y - LOW
    row = lax.broadcasted_iota(jnp.int32, (rows, width), 0)
    column = lax.broadcasted_iota(jnp.int32, (rows, width), 1)
    glob_y = row + first_y
    rows_in = (glob_y >= 0) & (glob_y < total_y)
    last_row = LOW + size_y + HIGH - 1
    field_in = rows_in & (row <= last_row)
    load_in = rows_in & (row >= 1) & (row < last_row)
    elements_in = rows_in & (glob_y < total_y - 1) & (row < last_row) & (column < width - 1)

    def left(v):
        return pltpu.roll(v, v.shape[1] - 1, 1)

    def right(v):
        return pltpu.roll(v, 1, 1)

    def lower(v):
        return pltpu.roll(v, v.shape[0] - 1, 0)

    def upper(v):
        return pltpu.roll(v, 1, 0)

    def stage(q, _):
        glob_z = q + first_z
        plane_in = (glob_z >= 0) & (glob_z < total_z)
        for c in range(3):
            cur[c, q] = jnp.where(field_in & plane_in, ext[c, q], 0.0)
        inner = plane_in & (glob_z < total_z - 1) & (q < planes - 1)
        emod[q] = jnp.where(elements_in & inner, ext[6, q], 0.0)
        return 0

    lax.fori_loop(0, planes, stage, 0)

    def sum_modes(q):
        e = emod[q]
        r = right(e)
        s, d = e + r, r - e
        us, ud = upper(s), upper(d)
        return s + us, us - s, d + ud, ud - d

    def invert(q, before):
        now = sum_modes(q)
        main = (LAME + 4.0 * SHEAR) / 9.0
        side = (LAME + SHEAR) / 12.0
        p = main * (now[0] + before[0])
        xy = side * (now[3] + before[3])
        xz = side * (before[2] - now[2])
        yz = side * (before[1] - now[1])
        pp = p * p
        c00 = pp - yz * yz
        c11 = pp - xz * xz
        c22 = pp - xy * xy
        c01 = xz * yz - xy * p
        c02 = xy * yz - xz * p
        c12 = xy * xz - yz * p
        det = p * c00 + xy * c01 + xz * c02
        scale = DAMPING / jnp.where(p > 0.0, det, 1.0)
        for k, entry in enumerate((c00, c11, c22, c01, c02, c12)):
            inverse[k, q] = entry * scale
        return now

    lax.fori_loop(1, planes - 1, invert, sum_modes(0))

    def forward(q, _):
        for c in range(3):
            u = cur[c, q]
            a = left(u)
            for x, t in enumerate((u + a, a - u)):
                b = lower(t)
                modes[4 * c + 2 * x, q] = t + b
                modes[4 * c + 2 * x + 1, q] = b - t
        return 0

    def apply(first, last, finish):
        lax.fori_loop(first - 1, last + 1, forward, 0)
        for tile in range(rows // 8):
            at = pl.ds(8 * tile, 8)

            def element(q, carry):
                lo = [
                    [[modes[4 * c + 2 * x + y, q, at] for y in range(2)] for x in range(2)]
                    for c in range(3)
                ]
                hi = [
                    [[modes[4 * c + 2 * x + y, q + 1, at] for y in range(2)] for x in range(2)]
                    for c in range(3)
                ]
                out = element_modes(lo, hi, emod[q, at])
                after = []
                for c in range(3):
                    for x in range(2):
                        for y in range(2):
                            k = 4 * c + 2 * x + y
                            total, change = out[c][x][y]
                            if total is None:
                                back[k, q, at] = carry[k] - change
                                after.append(change)
                            else:
                                back[k, q, at] = carry[k] + (total - change)
                                after.append(total + change)
                return tuple(after)

            zero = jnp.zeros((8, width), F32)
            carry = element(first - 1, (zero,) * 12)
            lax.fori_loop(first, last, element, carry, unroll=unroll)

        def gather(q, _):
            image = []
            for c in range(3):
                halves = []
                for x in range(2):
                    s, d = back[4 * c + 2 * x, q], back[4 * c + 2 * x + 1, q]
                    halves.append((s - d) + upper(s + d))
                s, d = halves
                image.append((s - d) + right(s + d))
            finish(q, image)
            return 0

        lax.fori_loop(first, last, gather, 0)

    def misfit(q, image):
        glob_z = q + first_z
        inside = load_in & (glob_z >= 0) & (glob_z < total_z)
        return [jnp.where(inside, ext[3 + c, q], 0.0) - image[c] for c in range(3)]

    def update(q, image):
        r0, r1, r2 = misfit(q, image)
        i00, i11, i22, i01, i02, i12 = [inverse[k, q] for k in range(6)]
        cur[0, q] += i00 * r0 + i01 * r1 + i02 * r2
        cur[1, q] += i01 * r0 + i11 * r1 + i12 * r2
        cur[2, q] += i02 * r0 + i12 * r1 + i22 * r2

    def keep(q, image):
        for c, value in enumerate(misfit(q, image)):
            resid[c, q] = value

    for sweep in range(SWEEPS):
        apply(sweep + 1, planes - 1 - sweep, update)
    apply(LOW, LOW + size_z + 1, keep)

    for c in range(3):
        for z in range(size_z):
            smooth[c, z] = cur[c, LOW + z, LOW : LOW + size_y]

    parts_z, parts_y, parts_x = coarse.shape[1], size_y // 4, width // 4
    seg_after_z = ext[6, planes - 1, 0:1, :]
    seg_after_y = ext[6, planes - 1, 1:2, :]
    maps = []
    for k in range(parts_z):
        want = slab * parts_z + k
        weights = []
        places = []
        for z in range(size_z):
            weights.append(jnp.where(seg_z[z] == want, 1.0, 0.0).astype(F32))
            places.append(0.5 * (slab * size_z + z - 4 * want - 2).astype(F32))
        count = sum(weights)
        moment = sum(w * p for w, p in zip(weights, places))
        last = jnp.where((seg_after_z == want.astype(F32)) & (slab < lax.axis_size("slab") - 1), 1.0, 0.0)
        place = 0.5 * ((slab + 1) * size_z - 4 * want - 2).astype(F32)
        weights.append(last)
        places.append(place)
        count = count + last
        centre = (moment + last * place) / count
        scale = lax.rsqrt(count)
        sums = [jnp.zeros((rows, width), F32) for _ in range(3)]
        turns = [jnp.zeros((rows, width), F32) for _ in range(2)]
        for z in range(size_z + 1):
            for c in range(3):
                part = weights[z] * resid[c, LOW + z]
                sums[c] = sums[c] + part
                if c < 2:
                    turns[c] = turns[c] + places[z] * part
        maps += [scale * s for s in sums]
        maps += [scale * (turns[c] - centre * sums[c]) for c in range(2)]

    lane = lax.broadcasted_iota(jnp.int32, (2 * parts_y, rows), 1)
    part = lax.broadcasted_iota(jnp.int32, (2 * parts_y, rows), 0)
    turned = part >= parts_y
    part = jnp.where(turned, part - parts_y, part) + sub * parts_y
    segments = jnp.full((2 * parts_y, rows), -1, jnp.int32)
    for y in range(size_y):
        segments = jnp.where(lane == LOW + y, seg_y[y], segments)
    after = jnp.broadcast_to(seg_after_y[:, :rows], segments.shape)
    hit = (lane == LOW + size_y) & (after == part.astype(F32)) & (sub < lax.axis_size("sub") - 1)
    weight_y = jnp.where((segments == part) | hit, 1.0, 0.0)
    place_y = 0.5 * (lane + first_y - 4 * part - 2).astype(F32)
    count = jnp.sum(weight_y, axis=1, keepdims=True)
    centre = jnp.sum(weight_y * place_y, axis=1, keepdims=True) / count
    weight_y = weight_y * lax.rsqrt(count) * jnp.where(turned, place_y - centre, 1.0)

    square = (parts_y * parts_x, width)
    part = lax.rem(lax.broadcasted_iota(jnp.int32, square, 0), parts_x)
    weight_x = jnp.where(seg_x[...] == part, 1.0, 0.0)
    place_x = 0.5 * (lax.broadcasted_iota(jnp.int32, square, 1) - 4 * part - 2).astype(F32)
    count = jnp.sum(weight_x, axis=1, keepdims=True)
    centre = jnp.sum(weight_x * place_x, axis=1, keepdims=True) / count
    weight_x = weight_x * lax.rsqrt(count)
    weight_x = jnp.concatenate([weight_x, weight_x * (place_x - centre)], axis=0)

    wide = jnp.concatenate(maps, axis=1)
    by_y = jnp.dot(
        weight_y, wide, precision=lax.Precision.HIGHEST, preferred_element_type=F32
    )
    tall = jnp.concatenate(
        [by_y[:, width * k : width * (k + 1)] for k in range(len(maps))], axis=0
    )
    by_x = lax.dot_general(
        tall,
        weight_x,
        (((1,), (1,)), ((), ())),
        precision=lax.Precision.HIGHEST,
        preferred_element_type=F32,
    )
    spread = parts_y * parts_x
    pick = lax.broadcasted_iota(jnp.int32, (parts_y, spread), 0) == (
        lax.broadcasted_iota(jnp.int32, (parts_y, spread), 1) // parts_x
    )

    def chosen(k, turn_y, turn_x):
        start = (2 * k + turn_y) * parts_y
        block = by_x[start : start + parts_y, turn_x * spread : (turn_x + 1) * spread]
        return jnp.sum(jnp.where(pick, block, 0.0), axis=0, keepdims=True)

    for k in range(parts_z):
        b = 5 * k
        values = [chosen(b, 0, 0), chosen(b + 1, 0, 0), chosen(b + 2, 0, 0)]
        values.append(chosen(b + 2, 1, 0) - chosen(b + 4, 0, 0))
        values.append(chosen(b + 3, 0, 0) - chosen(b + 2, 0, 1))
        values.append(chosen(b + 1, 0, 1) - chosen(b, 1, 0))
        for c in range(6):
            coarse[c, k : k + 1, :] = values[c]


def on_device(field_init, load, modulus, seg_z, seg_y, seg_x):
    size_z, size_y, width = modulus.shape
    planes = size_z + LOW + HIGH
    rows = -(-(size_y + LOW + HIGH) // 8) * 8
    any_space = pl.BlockSpec(memory_space=pl.ANY)
    smem = pl.BlockSpec(memory_space=pltpu.SMEM)
    vmem = pl.BlockSpec(memory_space=pltpu.VMEM)
    ext = pl.pallas_call(
        halo_kernel,
        out_shape=jax.ShapeDtypeStruct((7, planes, rows, 1, width), F32),
        in_specs=[any_space, any_space, any_space, smem, smem],
        out_specs=any_space,
        scratch_shapes=[
            pltpu.VMEM((2, 1, width), F32),
            pltpu.SemaphoreType.DMA((len(SIDES), 4)),
            pltpu.SemaphoreType.DMA((len(SIDES), 4)),
            pltpu.SemaphoreType.DMA((3,)),
        ],
        compiler_params=pltpu.CompilerParams(collective_id=0, has_side_effects=True),
        name="halo",
    )(
        field_init.reshape(3, size_z, size_y, 1, width),
        load.reshape(3, size_z, size_y, 1, width),
        modulus.reshape(size_z, size_y, 1, width),
        seg_z,
        seg_y,
    )
    ext = ext.reshape(7, planes, rows, width)
    block = (planes, rows, width)
    smooth, coarse = pl.pallas_call(
        functools.partial(compute_kernel, unroll=1),
        out_shape=(
            jax.ShapeDtypeStruct((3, size_z, size_y, width), F32),
            jax.ShapeDtypeStruct((6, size_z // 4, size_y * width // 16), F32),
        ),
        in_specs=[smem, smem, vmem, vmem],
        out_specs=(vmem, vmem),
        scratch_shapes=[
            pltpu.VMEM((3, *block), F32),
            pltpu.VMEM(block, F32),
            pltpu.VMEM((6, *block), F32),
            pltpu.VMEM((12, *block), F32),
            pltpu.VMEM((12, *block), F32),
            pltpu.VMEM((3, *block), F32),
        ],
        compiler_params=pltpu.CompilerParams(vmem_limit_bytes=32 << 20),
        name="sweeps",
    )(seg_z, seg_y, seg_x.reshape(1, width), ext)
    return smooth, coarse


def solution(mesh):
    in_specs = (
        P(None, "slab", "sub", None),
        P(None, "slab", "sub", None),
        P("slab", "sub", None),
        P("slab"),
        P("sub"),
        P(),
    )
    out_specs = (P(None, "slab", "sub", None), P(None, "slab", "sub"))
    return jax.shard_map(
        on_device, mesh=mesh, in_specs=in_specs, out_specs=out_specs, check_vma=False
    )
```

```python
import functools

import jax
import jax.numpy as jnp
from jax import lax
from jax.experimental import pallas as pl
from jax.experimental.pallas import tpu as pltpu
from jax.sharding import PartitionSpec as P

SWEEPS = 2
DAMPING = 0.6
PAD = 4
REACH = ((SWEEPS + 1, SWEEPS + 2), (SWEEPS, SWEEPS + 1), (SWEEPS + 1, SWEEPS + 1))
POISSON = 0.3
LAME = POISSON / ((1.0 + POISSON) * (1.0 - 2.0 * POISSON))
SHEAR = 0.5 / (1.0 + POISSON)
SIDES = ((-1, 0), (1, 0), (0, -1), (0, 1), (-1, -1), (-1, 1), (1, -1), (1, 1))
UNROLL = 2
MESH = pl.DeviceIdType.MESH
F32 = jnp.float32


def element_modes(lo, hi, e):
    def up(c, x, y):
        return lo[c][x][y] + hi[c][x][y]

    def diff(c, x, y):
        return hi[c][x][y] - lo[c][x][y]

    e_shear = e * (SHEAR / 16.0)
    e_shear2 = e * (SHEAR / 8.0)
    e_lame = e * (LAME / 16.0)
    e_lame3 = e * (LAME / 48.0)
    e_shear3 = e * (SHEAR / 48.0)
    e_last = e * ((LAME + 4.0 * SHEAR) / 144.0)
    out = [[[[None, None], [None, None]] for _ in range(2)] for _ in range(3)]

    n0, n1, n2 = up(0, 1, 0), up(1, 0, 1), diff(2, 0, 0)
    both = e_lame * (n0 + n1 + n2)
    out[0][1][0][0] = both + e_shear2 * n0
    out[1][0][1][0] = both + e_shear2 * n1
    out[2][0][0][1] = both + e_shear2 * n2

    both = e_shear * (up(0, 0, 1) + up(1, 1, 0))
    out[0][0][1][0] = both
    out[1][1][0][0] = both
    both = e_shear * (diff(0, 0, 0) + up(2, 1, 0))
    out[0][0][0][1] = both
    out[2][1][0][0] = both
    both = e_shear * (diff(1, 0, 0) + up(2, 0, 1))
    out[1][0][0][1] = both
    out[2][0][1][0] = both

    a, b = up(0, 1, 1), diff(2, 0, 1)
    both = e_lame3 * (a + b)
    out[0][1][1][0] = both + e_shear * a
    out[2][0][1][1] = both + e_shear * b
    a, b = diff(0, 1, 0), diff(1, 0, 1)
    both = e_lame3 * (a + b)
    out[0][1][0][1] = both + e_shear * a
    out[1][0][1][1] = both + e_shear * b
    a, b = up(1, 1, 1), diff(2, 1, 0)
    both = e_lame3 * (a + b)
    out[1][1][1][0] = both + e_shear * a
    out[2][1][0][1] = both + e_shear * b

    a, b, c = diff(0, 0, 1), diff(1, 1, 0), up(2, 1, 1)
    both = a + b + c
    out[0][0][1][1] = e_shear3 * (both + a)
    out[1][1][0][1] = e_shear3 * (both + b)
    out[2][1][1][0] = e_shear3 * (both + c)

    for c in range(3):
        out[c][1][1][1] = e_last * diff(c, 1, 1)
    return out


def kernel(
    seg_z,
    seg_y,
    seg_x,
    field,
    load,
    mod,
    smooth,
    coarse,
    packed,
    tails,
    halo,
    mark,
    marked,
    weights_x,
    cur,
    right_side,
    emod,
    inverse,
    modes,
    back,
    resid,
    send_sem,
    recv_sem,
    *,
    unroll,
):
    size_z, size_y, width = smooth.shape[1:]
    planes, rows = cur.shape[1], cur.shape[2]
    slab, sub = lax.axis_index("slab"), lax.axis_index("sub")
    slabs, subs = lax.axis_size("slab"), lax.axis_size("sub")
    total_z, total_y = size_z * slabs, size_y * subs
    parts_z, parts_y, parts_x = size_z // 4, size_y // 4, width // 4
    pairs = PAD // 2
    own_pairs = size_z // 2

    def present(dz, dy):
        there = jnp.bool_(True)
        if dz == 1:
            there = there & (slab < slabs - 1)
        if dz == -1:
            there = there & (slab > 0)
        if dy == 1:
            there = there & (sub < subs - 1)
        if dy == -1:
            there = there & (sub > 0)
        return there

    barrier = pltpu.get_barrier_semaphore()
    for dz, dy in SIDES:

        @pl.when(present(dz, dy))
        def _():
            pl.semaphore_signal(
                barrier, inc=1, device_id=(slab + dz, sub + dy), device_id_type=MESH
            )

    first_half = lax.broadcasted_iota(jnp.int32, (8, width), 0) < PAD

    def unit(refs, k):
        return refs[k // 3].at[k % 3] if k < 6 else refs[2]

    inputs = (field, load, mod)

    def pack(i, _):
        for k in range(7):
            src = unit(inputs, k)
            a, b = src[2 * i, 0:8], src[2 * i + 1, 0:8]
            packed[0, k, i] = jnp.where(first_half, a, pltpu.roll(b, PAD, 0))
            a, b = src[2 * i, size_y - 8 : size_y], src[2 * i + 1, size_y - 8 : size_y]
            packed[1, k, i] = jnp.where(first_half, pltpu.roll(b, PAD, 0), a)
        return 0

    lax.fori_loop(0, own_pairs, pack, 0)
    mark[0] = jnp.full((8, width), seg_z[0].astype(F32))
    mark[1] = jnp.full((8, width), seg_y[0].astype(F32))

    peers_z = 3 - (slab == 0).astype(jnp.int32) - (slab == slabs - 1).astype(jnp.int32)
    peers_y = 3 - (sub == 0).astype(jnp.int32) - (sub == subs - 1).astype(jnp.int32)
    pl.semaphore_wait(barrier, peers_z * peers_y - 1)

    copies = {}
    for side, (dz, dy) in enumerate(SIDES):
        group = []
        if dy == 0:
            for k, src in enumerate(inputs):
                low, high = REACH[k]
                if dz == 1:
                    start, to, count = size_z - low, PAD - low, low
                else:
                    start, to, count = 0, PAD + size_z, high
                if k < 2:
                    group.append(
                        (
                            src.at[:, pl.ds(start, count)],
                            halo.at[pl.ds(3 * k, 3), pl.ds(to, count)],
                        )
                    )
                else:
                    group.append((src.at[pl.ds(start, count)], halo.at[6, pl.ds(to, count)]))
        else:
            which = 0 if dy == -1 else 1
            start, to, count = {
                -1: (0, pairs + own_pairs, pairs),
                0: (0, pairs, own_pairs),
                1: (own_pairs - pairs, 0, pairs),
            }[dz]
            group.append(
                (
                    packed.at[which, :, pl.ds(start, count)],
                    tails.at[which, :, pl.ds(to, count)],
                )
            )
        if (dz, dy) == (-1, 0):
            group.append((mark.at[0], marked.at[0]))
        if (dz, dy) == (0, -1):
            group.append((mark.at[1], marked.at[1]))
        group = [
            pltpu.make_async_remote_copy(
                src_ref=from_ref,
                dst_ref=to_ref,
                send_sem=send_sem.at[side, k],
                recv_sem=recv_sem.at[side, k],
                device_id=(slab + dz, sub + dy),
                device_id_type=MESH,
            )
            for k, (from_ref, to_ref) in enumerate(group)
        ]
        copies[dz, dy] = group

        @pl.when(present(dz, dy))
        def _():
            for copy in group:
                copy.start()

    def arrived(sides):
        for dz, dy in sides:

            @pl.when(present(-dz, -dy))
            def _():
                for copy in copies[dz, dy]:
                    copy.wait_recv()

    square = (parts_y * parts_x, width)
    part = lax.rem(lax.broadcasted_iota(jnp.int32, square, 0), parts_x)
    weight_x = jnp.where(seg_x[...] == part, 1.0, 0.0)
    place_x = 0.5 * (lax.broadcasted_iota(jnp.int32, square, 1) - 4 * part - 2).astype(F32)
    count = jnp.sum(weight_x, axis=1, keepdims=True)
    centre = jnp.sum(weight_x * place_x, axis=1, keepdims=True) / count
    weight_x = weight_x * lax.rsqrt(count)
    weights_x[0 : square[0]] = weight_x
    weights_x[square[0] : 2 * square[0]] = weight_x * (place_x - centre)

    first_z = slab * size_z - PAD
    row = lax.broadcasted_iota(jnp.int32, (rows, width), 0)
    column = lax.broadcasted_iota(jnp.int32, (rows, width), 1)
    near = jnp.where(row < size_y + PAD, row, row - rows)
    glob_y = near + sub * size_y
    rows_in = (glob_y >= 0) & (glob_y < total_y)
    elements_in = (
        rows_in
        & (glob_y < total_y - 1)
        & (near >= -SWEEPS - 1)
        & (near < size_y + SWEEPS + 1)
        & (column < width - 1)
    )

    def left(v):
        return pltpu.roll(v, v.shape[1] - 1, 1)

    def right(v):
        return pltpu.roll(v, 1, 1)

    def lower(v):
        return pltpu.roll(v, v.shape[0] - 1, 0)

    def upper(v):
        return pltpu.roll(v, 1, 0)

    def stage(i, refs, shift):
        for k in range(7):
            src = unit(refs, k) if shift else halo.at[k]
            above, below = tails[0, k, i], tails[1, k, i]
            ends = (
                jnp.where(first_half, above, below),
                pltpu.roll(jnp.where(first_half, below, above), PAD, 0),
            )
            for odd in range(2):
                q = 2 * i + odd
                glob_z = q + first_z
                value = jnp.concatenate([src[q - shift], ends[odd]], axis=0)
                if k < 6:
                    keep = rows_in & (glob_z >= 0) & (glob_z < total_z)
                    value = jnp.where(keep, value, 0.0)
                    if k < 3:
                        cur[k, q] = value
                    else:
                        right_side[k - 3, q] = value
                else:
                    keep = elements_in & (glob_z >= 0) & (glob_z < total_z - 1)
                    emod[q] = jnp.where(keep, value, 0.0)

    def stage_own(i, _):
        stage(i, inputs, PAD)
        return 0

    def stage_halo(i, _):
        stage(i, None, 0)
        return 0

    def sum_modes(q):
        e = emod[q]
        r = right(e)
        s, d = e + r, r - e
        us, ud = upper(s), upper(d)
        return s + us, us - s, d + ud, ud - d

    def invert(q, before):
        now = sum_modes(q)
        main = (LAME + 4.0 * SHEAR) / 9.0
        side = (LAME + SHEAR) / 12.0
        p = main * (now[0] + before[0])
        xy = side * (now[3] + before[3])
        xz = side * (before[2] - now[2])
        yz = side * (before[1] - now[1])
        pp = p * p
        c00 = pp - yz * yz
        c11 = pp - xz * xz
        c22 = pp - xy * xy
        c01 = xz * yz - xy * p
        c02 = xy * yz - xz * p
        c12 = xy * xz - yz * p
        det = p * c00 + xy * c01 + xz * c02
        scale = DAMPING / jnp.where(p > 0.0, det, 1.0)
        for k, entry in enumerate((c00, c11, c22, c01, c02, c12)):
            inverse[k, q] = entry * scale
        return now

    def forward(q, _):
        for c in range(3):
            u = cur[c, q]
            a = left(u)
            for x, t in enumerate((u + a, a - u)):
                b = lower(t)
                modes[4 * c + 2 * x, q] = t + b
                modes[4 * c + 2 * x + 1, q] = b - t
        return 0

    tiles = [pl.ds(8 * tile, 8) for tile in range(rows // 8)]

    def elements(first, last, begin):
        for at in tiles:

            def element(q, carry):
                lo = [
                    [[modes[4 * c + 2 * x + y, q, at] for y in range(2)] for x in range(2)]
                    for c in range(3)
                ]
                hi = [
                    [[modes[4 * c + 2 * x + y, q + 1, at] for y in range(2)] for x in range(2)]
                    for c in range(3)
                ]
                out = element_modes(lo, hi, emod[q, at])
                after = []
                for c in range(3):
                    for x in range(2):
                        for y in range(2):
                            k = 4 * c + 2 * x + y
                            total, change = out[c][x][y]
                            if total is None:
                                back[k, q, at] = carry[k] - change
                                after.append(change)
                            else:
                                back[k, q, at] = carry[k] + (total - change)
                                after.append(total + change)
                return tuple(after)

            if begin:
                carry = tuple(back[k, first, at] for k in range(12))
            else:
                carry = (jnp.zeros((8, width), F32),) * 12
            carry = lax.fori_loop(first, last, element, carry, unroll=unroll)
            for k in range(12):
                back[k, last, at] = carry[k]

    def image(q):
        result = []
        for c in range(3):
            halves = []
            for x in range(2):
                s, d = back[4 * c + 2 * x, q], back[4 * c + 2 * x + 1, q]
                halves.append((s - d) + upper(s + d))
            s, d = halves
            result.append((s - d) + right(s + d))
        return result

    def misfit(q):
        moved = image(q)
        return [right_side[c, q] - moved[c] for c in range(3)]

    def update(q, _):
        r0, r1, r2 = misfit(q)
        i00, i11, i22, i01, i02, i12 = [inverse[k, q] for k in range(6)]
        cur[0, q] += i00 * r0 + i01 * r1 + i02 * r2
        cur[1, q] += i01 * r0 + i11 * r1 + i12 * r2
        cur[2, q] += i02 * r0 + i12 * r1 + i22 * r2
        return forward(q, 0)

    def keep(q, _):
        for c, value in enumerate(misfit(q)):
            resid[c, q] = value
        return 0

    top = PAD + size_z
    arrived([(0, -1), (0, 1)])
    lax.fori_loop(pairs, pairs + own_pairs, stage_own, 0)
    lax.fori_loop(PAD, top, forward, 0)
    elements(PAD, top - 1, False)
    lax.fori_loop(PAD + 1, top - 1, invert, sum_modes(PAD))
    arrived([side for side in SIDES if side[0] != 0])
    lax.fori_loop(0, pairs, stage_halo, 0)
    lax.fori_loop(pairs + own_pairs, 2 * pairs + own_pairs, stage_halo, 0)
    lax.fori_loop(1, PAD, forward, 0)
    lax.fori_loop(top, planes, forward, 0)
    held = [[back[k, PAD, at] for at in tiles] for k in range(12)]
    elements(1, PAD, False)
    for k in range(12):
        for at, value in zip(tiles, held[k]):
            back[k, PAD, at] += value
    elements(top - 1, planes - 1, True)
    lax.fori_loop(2, PAD + 1, invert, sum_modes(1))
    lax.fori_loop(top - 1, planes - 1, invert, sum_modes(top - 2))
    lax.fori_loop(2, planes - 1, update, 0)
    for sweep in range(1, SWEEPS):
        elements(sweep + 1, planes - 1 - sweep, False)
        lax.fori_loop(sweep + 2, planes - 1 - sweep, update, 0)
    elements(PAD - 1, top + 1, False)
    lax.fori_loop(PAD, top + 1, keep, 0)
    for c in range(3):
        for z in range(size_z):
            smooth[c, z] = cur[c, PAD + z, 0:size_y]

    seg_after_z = marked[0, 0:1, :]
    seg_after_y = marked[1, 0:1, :]
    maps = []
    for k in range(parts_z):
        want = slab * parts_z + k
        weights = []
        places = []
        for z in range(size_z):
            weights.append(jnp.where(seg_z[z] == want, 1.0, 0.0).astype(F32))
            places.append(0.5 * (slab * size_z + z - 4 * want - 2).astype(F32))
        count = sum(weights)
        moment = sum(w * p for w, p in zip(weights, places))
        last = jnp.where((seg_after_z == want.astype(F32)) & (slab < slabs - 1), 1.0, 0.0)
        place = 0.5 * ((slab + 1) * size_z - 4 * want - 2).astype(F32)
        weights.append(last)
        places.append(place)
        count = count + last
        centre = (moment + last * place) / count
        scale = lax.rsqrt(count)
        sums = [jnp.zeros((rows, width), F32) for _ in range(3)]
        turns = [jnp.zeros((rows, width), F32) for _ in range(2)]
        for z in range(size_z + 1):
            for c in range(3):
                part = weights[z] * resid[c, PAD + z]
                sums[c] = sums[c] + part
                if c < 2:
                    turns[c] = turns[c] + places[z] * part
        maps += [scale * s for s in sums]
        maps += [scale * (turns[c] - centre * sums[c]) for c in range(2)]

    lane = lax.broadcasted_iota(jnp.int32, (2 * parts_y, rows), 1)
    part = lax.broadcasted_iota(jnp.int32, (2 * parts_y, rows), 0)
    turned = part >= parts_y
    part = jnp.where(turned, part - parts_y, part) + sub * parts_y
    segments = jnp.full((2 * parts_y, rows), -1, jnp.int32)
    for y in range(size_y):
        segments = jnp.where(lane == y, seg_y[y], segments)
    after = jnp.broadcast_to(seg_after_y[:, :rows], segments.shape)
    hit = (lane == size_y) & (after == part.astype(F32)) & (sub < subs - 1)
    weight_y = jnp.where((segments == part) | hit, 1.0, 0.0)
    place_y = 0.5 * (lane + sub * size_y - 4 * part - 2).astype(F32)
    count = jnp.sum(weight_y, axis=1, keepdims=True)
    centre = jnp.sum(weight_y * place_y, axis=1, keepdims=True) / count
    weight_y = weight_y * lax.rsqrt(count) * jnp.where(turned, place_y - centre, 1.0)

    wide = jnp.concatenate(maps, axis=1)
    by_y = jnp.dot(
        weight_y, wide, precision=lax.Precision.HIGHEST, preferred_element_type=F32
    )
    tall = jnp.concatenate(
        [by_y[:, width * k : width * (k + 1)] for k in range(len(maps))], axis=0
    )
    by_x = lax.dot_general(
        tall,
        weights_x[...],
        (((1,), (1,)), ((), ())),
        precision=lax.Precision.HIGHEST,
        preferred_element_type=F32,
    )
    spread = parts_y * parts_x
    pick = lax.broadcasted_iota(jnp.int32, (parts_y, spread), 0) == (
        lax.broadcasted_iota(jnp.int32, (parts_y, spread), 1) // parts_x
    )

    def chosen(k, turn_y, turn_x):
        start = (2 * k + turn_y) * parts_y
        block = by_x[start : start + parts_y, turn_x * spread : (turn_x + 1) * spread]
        return jnp.sum(jnp.where(pick, block, 0.0), axis=0, keepdims=True)

    for k in range(parts_z):
        b = 5 * k
        values = [chosen(b, 0, 0), chosen(b + 1, 0, 0), chosen(b + 2, 0, 0)]
        values.append(chosen(b + 2, 1, 0) - chosen(b + 4, 0, 0))
        values.append(chosen(b + 3, 0, 0) - chosen(b + 2, 0, 1))
        values.append(chosen(b + 1, 0, 1) - chosen(b, 1, 0))
        for c in range(6):
            coarse[c, k : k + 1, :] = values[c]

    for dz, dy in SIDES:

        @pl.when(present(dz, dy))
        def _():
            for copy in copies[dz, dy]:
                copy.wait_send()


def on_device(field_init, load, modulus, seg_z, seg_y, seg_x):
    size_z, size_y, width = modulus.shape
    planes = size_z + 2 * PAD
    rows = size_y + 2 * PAD
    smem = pl.BlockSpec(memory_space=pltpu.SMEM)
    vmem = pl.BlockSpec(memory_space=pltpu.VMEM)
    block = (planes, rows, width)
    smooth, coarse = pl.pallas_call(
        functools.partial(kernel, unroll=UNROLL),
        out_shape=(
            jax.ShapeDtypeStruct((3, size_z, size_y, width), F32),
            jax.ShapeDtypeStruct((6, size_z // 4, size_y * width // 16), F32),
        ),
        in_specs=[smem, smem, vmem, vmem, vmem, vmem],
        out_specs=(vmem, vmem),
        scratch_shapes=[
            pltpu.VMEM((2, 7, size_z // 2, 8, width), F32),
            pltpu.VMEM((2, 7, planes // 2, 8, width), F32),
            pltpu.VMEM((7, planes, size_y, width), F32),
            pltpu.VMEM((2, 8, width), F32),
            pltpu.VMEM((2, 8, width), F32),
            pltpu.VMEM((size_y * width // 8, width), F32),
            pltpu.VMEM((3, *block), F32),
            pltpu.VMEM((3, *block), F32),
            pltpu.VMEM(block, F32),
            pltpu.VMEM((6, *block), F32),
            pltpu.VMEM((12, *block), F32),
            pltpu.VMEM((12, *block), F32),
            pltpu.VMEM((3, *block), F32),
            pltpu.SemaphoreType.DMA((len(SIDES), 4)),
            pltpu.SemaphoreType.DMA((len(SIDES), 4)),
        ],
        compiler_params=pltpu.CompilerParams(
            collective_id=0, has_side_effects=True, vmem_limit_bytes=32 << 20
        ),
        name="sweeps",
    )(seg_z, seg_y, seg_x.reshape(1, width), field_init, load, modulus)
    return smooth, coarse


def solution(mesh):
    in_specs = (
        P(None, "slab", "sub", None),
        P(None, "slab", "sub", None),
        P("slab", "sub", None),
        P("slab"),
        P("sub"),
        P(),
    )
    out_specs = (P(None, "slab", "sub", None), P(None, "slab", "sub"))
    return jax.shard_map(
        on_device, mesh=mesh, in_specs=in_specs, out_specs=out_specs, check_vma=False
    )
```

```python
import functools

import jax
import jax.numpy as jnp
from jax import lax
from jax.experimental import pallas as pl
from jax.experimental.pallas import tpu as pltpu
from jax.sharding import PartitionSpec as P

SWEEPS = 2
DAMPING = 0.6
PAD = 4
REACH = ((SWEEPS + 1, SWEEPS + 2), (SWEEPS, SWEEPS + 1), (SWEEPS + 1, SWEEPS + 1))
POISSON = 0.3
LAME = POISSON / ((1.0 + POISSON) * (1.0 - 2.0 * POISSON))
SHEAR = 0.5 / (1.0 + POISSON)
SIDES = ((-1, 0), (1, 0), (0, -1), (0, 1), (-1, -1), (-1, 1), (1, -1), (1, 1))
UNROLL = 2
MESH = pl.DeviceIdType.MESH
F32 = jnp.float32


def element_modes(lo, hi, e):
    def up(c, x, y):
        return lo[c][x][y] + hi[c][x][y]

    def diff(c, x, y):
        return hi[c][x][y] - lo[c][x][y]

    e_shear = e * (SHEAR / 16.0)
    e_shear2 = e * (SHEAR / 8.0)
    e_lame = e * (LAME / 16.0)
    e_lame3 = e * (LAME / 48.0)
    e_shear3 = e * (SHEAR / 48.0)
    e_last = e * ((LAME + 4.0 * SHEAR) / 144.0)
    out = [[[[None, None], [None, None]] for _ in range(2)] for _ in range(3)]

    n0, n1, n2 = up(0, 1, 0), up(1, 0, 1), diff(2, 0, 0)
    both = e_lame * (n0 + n1 + n2)
    out[0][1][0][0] = both + e_shear2 * n0
    out[1][0][1][0] = both + e_shear2 * n1
    out[2][0][0][1] = both + e_shear2 * n2

    both = e_shear * (up(0, 0, 1) + up(1, 1, 0))
    out[0][0][1][0] = both
    out[1][1][0][0] = both
    both = e_shear * (diff(0, 0, 0) + up(2, 1, 0))
    out[0][0][0][1] = both
    out[2][1][0][0] = both
    both = e_shear * (diff(1, 0, 0) + up(2, 0, 1))
    out[1][0][0][1] = both
    out[2][0][1][0] = both

    a, b = up(0, 1, 1), diff(2, 0, 1)
    both = e_lame3 * (a + b)
    out[0][1][1][0] = both + e_shear * a
    out[2][0][1][1] = both + e_shear * b
    a, b = diff(0, 1, 0), diff(1, 0, 1)
    both = e_lame3 * (a + b)
    out[0][1][0][1] = both + e_shear * a
    out[1][0][1][1] = both + e_shear * b
    a, b = up(1, 1, 1), diff(2, 1, 0)
    both = e_lame3 * (a + b)
    out[1][1][1][0] = both + e_shear * a
    out[2][1][0][1] = both + e_shear * b

    a, b, c = diff(0, 0, 1), diff(1, 1, 0), up(2, 1, 1)
    both = a + b + c
    out[0][0][1][1] = e_shear3 * (both + a)
    out[1][1][0][1] = e_shear3 * (both + b)
    out[2][1][1][0] = e_shear3 * (both + c)

    for c in range(3):
        out[c][1][1][1] = e_last * diff(c, 1, 1)
    return out


def flat(first, last, body, carry=0):
    for q in range(first, last):
        carry = body(q, carry)
    return carry


def kernel(
    seg_z_hbm,
    seg_y_hbm,
    seg_x_hbm,
    field_hbm,
    load_hbm,
    mod_hbm,
    smooth,
    coarse,
    seg_z,
    seg_y,
    seg_x,
    field,
    load,
    mod,
    own_sem,
    packed,
    tails,
    halo,
    mark,
    marked,
    weights_x,
    cur,
    right_side,
    emod,
    inverse,
    modes,
    back,
    resid,
    send_sem,
    recv_sem,
    *,
    unroll,
):
    size_z, size_y, width = smooth.shape[1:]
    planes, rows = cur.shape[1], cur.shape[2]
    slab, sub = lax.axis_index("slab"), lax.axis_index("sub")
    slabs, subs = lax.axis_size("slab"), lax.axis_size("sub")
    total_z, total_y = size_z * slabs, size_y * subs
    parts_z, parts_y, parts_x = size_z // 4, size_y // 4, width // 4
    pairs = PAD // 2
    own_pairs = size_z // 2

    def present(dz, dy):
        there = jnp.bool_(True)
        if dz == 1:
            there = there & (slab < slabs - 1)
        if dz == -1:
            there = there & (slab > 0)
        if dy == 1:
            there = there & (sub < subs - 1)
        if dy == -1:
            there = there & (sub > 0)
        return there

    barrier = pltpu.get_barrier_semaphore()
    for dz, dy in SIDES:

        @pl.when(present(dz, dy))
        def _():
            pl.semaphore_signal(
                barrier, inc=1, device_id=(slab + dz, sub + dy), device_id_type=MESH
            )

    own = [
        pltpu.make_async_copy(src, dst, own_sem.at[k])
        for k, (src, dst) in enumerate(
            (
                (field_hbm, field),
                (load_hbm, load),
                (mod_hbm, mod),
                (seg_z_hbm, seg_z),
                (seg_y_hbm, seg_y),
                (seg_x_hbm, seg_x),
            )
        )
    ]
    for copy in own:
        copy.start()
    for copy in own:
        copy.wait()

    first_half = lax.broadcasted_iota(jnp.int32, (8, width), 0) < PAD

    def unit(refs, k):
        return refs[k // 3].at[k % 3] if k < 6 else refs[2]

    inputs = (field, load, mod)

    def pack(i, _):
        for k in range(7):
            src = unit(inputs, k)
            a, b = src[2 * i, 0:8], src[2 * i + 1, 0:8]
            packed[0, k, i] = jnp.where(first_half, a, pltpu.roll(b, PAD, 0))
            a, b = src[2 * i, size_y - 8 : size_y], src[2 * i + 1, size_y - 8 : size_y]
            packed[1, k, i] = jnp.where(first_half, pltpu.roll(b, PAD, 0), a)
        return 0

    flat(0, own_pairs, pack)
    mark[0] = jnp.full((8, width), seg_z[0].astype(F32))
    mark[1] = jnp.full((8, width), seg_y[0].astype(F32))

    peers_z = 3 - (slab == 0).astype(jnp.int32) - (slab == slabs - 1).astype(jnp.int32)
    peers_y = 3 - (sub == 0).astype(jnp.int32) - (sub == subs - 1).astype(jnp.int32)
    pl.semaphore_wait(barrier, peers_z * peers_y - 1)

    copies = {}
    for side, (dz, dy) in enumerate(SIDES):
        group = []
        if dy == 0:
            for k, src in enumerate(inputs):
                low, high = REACH[k]
                if dz == 1:
                    start, to, count = size_z - low, PAD - low, low
                else:
                    start, to, count = 0, PAD + size_z, high
                if k < 2:
                    group.append(
                        (
                            src.at[:, pl.ds(start, count)],
                            halo.at[pl.ds(3 * k, 3), pl.ds(to, count)],
                        )
                    )
                else:
                    group.append((src.at[pl.ds(start, count)], halo.at[6, pl.ds(to, count)]))
        else:
            which = 0 if dy == -1 else 1
            start, to, count = {
                -1: (0, pairs + own_pairs, pairs),
                0: (0, pairs, own_pairs),
                1: (own_pairs - pairs, 0, pairs),
            }[dz]
            group.append(
                (
                    packed.at[which, :, pl.ds(start, count)],
                    tails.at[which, :, pl.ds(to, count)],
                )
            )
        if (dz, dy) == (-1, 0):
            group.append((mark.at[0], marked.at[0]))
        if (dz, dy) == (0, -1):
            group.append((mark.at[1], marked.at[1]))
        group = [
            pltpu.make_async_remote_copy(
                src_ref=from_ref,
                dst_ref=to_ref,
                send_sem=send_sem.at[side, k],
                recv_sem=recv_sem.at[side, k],
                device_id=(slab + dz, sub + dy),
                device_id_type=MESH,
            )
            for k, (from_ref, to_ref) in enumerate(group)
        ]
        copies[dz, dy] = group

        @pl.when(present(dz, dy))
        def _():
            for copy in group:
                copy.start()

    def arrived(sides):
        for dz, dy in sides:

            @pl.when(present(-dz, -dy))
            def _():
                for copy in copies[dz, dy]:
                    copy.wait_recv()

    square = (parts_y * parts_x, width)
    part = lax.rem(lax.broadcasted_iota(jnp.int32, square, 0), parts_x)
    weight_x = jnp.where(seg_x[...] == part, 1.0, 0.0)
    place_x = 0.5 * (lax.broadcasted_iota(jnp.int32, square, 1) - 4 * part - 2).astype(F32)
    count = jnp.sum(weight_x, axis=1, keepdims=True)
    centre = jnp.sum(weight_x * place_x, axis=1, keepdims=True) / count
    weight_x = weight_x * lax.rsqrt(count)
    weights_x[0 : square[0]] = weight_x
    weights_x[square[0] : 2 * square[0]] = weight_x * (place_x - centre)

    first_z = slab * size_z - PAD
    row = lax.broadcasted_iota(jnp.int32, (rows, width), 0)
    column = lax.broadcasted_iota(jnp.int32, (rows, width), 1)
    near = jnp.where(row < size_y + PAD, row, row - rows)
    glob_y = near + sub * size_y
    rows_in = (glob_y >= 0) & (glob_y < total_y)
    elements_in = (
        rows_in
        & (glob_y < total_y - 1)
        & (near >= -SWEEPS - 1)
        & (near < size_y + SWEEPS + 1)
        & (column < width - 1)
    )

    def left(v):
        return pltpu.roll(v, v.shape[1] - 1, 1)

    def right(v):
        return pltpu.roll(v, 1, 1)

    def lower(v):
        return pltpu.roll(v, v.shape[0] - 1, 0)

    def upper(v):
        return pltpu.roll(v, 1, 0)

    def stage(i, refs, shift):
        for k in range(7):
            src = unit(refs, k) if shift else halo.at[k]
            above, below = tails[0, k, i], tails[1, k, i]
            ends = (
                jnp.where(first_half, above, below),
                pltpu.roll(jnp.where(first_half, below, above), PAD, 0),
            )
            for odd in range(2):
                q = 2 * i + odd
                glob_z = q + first_z
                value = jnp.concatenate([src[q - shift], ends[odd]], axis=0)
                if k < 6:
                    keep = rows_in & (glob_z >= 0) & (glob_z < total_z)
                    value = jnp.where(keep, value, 0.0)
                    if k < 3:
                        cur[k, q] = value
                    else:
                        right_side[k - 3, q] = value
                else:
                    keep = elements_in & (glob_z >= 0) & (glob_z < total_z - 1)
                    emod[q] = jnp.where(keep, value, 0.0)

    def stage_own(i, _):
        stage(i, inputs, PAD)
        return 0

    def stage_halo(i, _):
        stage(i, None, 0)
        return 0

    def sum_modes(q):
        e = emod[q]
        r = right(e)
        s, d = e + r, r - e
        us, ud = upper(s), upper(d)
        return s + us, us - s, d + ud, ud - d

    def invert(q, before):
        now = sum_modes(q)
        main = (LAME + 4.0 * SHEAR) / 9.0
        side = (LAME + SHEAR) / 12.0
        p = main * (now[0] + before[0])
        xy = side * (now[3] + before[3])
        xz = side * (before[2] - now[2])
        yz = side * (before[1] - now[1])
        pp = p * p
        c00 = pp - yz * yz
        c11 = pp - xz * xz
        c22 = pp - xy * xy
        c01 = xz * yz - xy * p
        c02 = xy * yz - xz * p
        c12 = xy * xz - yz * p
        det = p * c00 + xy * c01 + xz * c02
        scale = DAMPING / jnp.where(p > 0.0, det, 1.0)
        for k, entry in enumerate((c00, c11, c22, c01, c02, c12)):
            inverse[k, q] = entry * scale
        return now

    def forward(q, _):
        for c in range(3):
            u = cur[c, q]
            a = left(u)
            for x, t in enumerate((u + a, a - u)):
                b = lower(t)
                modes[4 * c + 2 * x, q] = t + b
                modes[4 * c + 2 * x + 1, q] = b - t
        return 0

    tiles = [pl.ds(8 * tile, 8) for tile in range(rows // 8)]

    def elements(first, last, begin):
        for at in tiles:

            def element(q, carry):
                lo = [
                    [[modes[4 * c + 2 * x + y, q, at] for y in range(2)] for x in range(2)]
                    for c in range(3)
                ]
                hi = [
                    [[modes[4 * c + 2 * x + y, q + 1, at] for y in range(2)] for x in range(2)]
                    for c in range(3)
                ]
                out = element_modes(lo, hi, emod[q, at])
                after = []
                for c in range(3):
                    for x in range(2):
                        for y in range(2):
                            k = 4 * c + 2 * x + y
                            total, change = out[c][x][y]
                            if total is None:
                                back[k, q, at] = carry[k] - change
                                after.append(change)
                            else:
                                back[k, q, at] = carry[k] + (total - change)
                                after.append(total + change)
                return tuple(after)

            if begin:
                carry = tuple(back[k, first, at] for k in range(12))
            else:
                carry = (jnp.zeros((8, width), F32),) * 12
            carry = lax.fori_loop(first, last, element, carry, unroll=unroll)
            for k in range(12):
                back[k, last, at] = carry[k]

    def image(q):
        result = []
        for c in range(3):
            halves = []
            for x in range(2):
                s, d = back[4 * c + 2 * x, q], back[4 * c + 2 * x + 1, q]
                halves.append((s - d) + upper(s + d))
            s, d = halves
            result.append((s - d) + right(s + d))
        return result

    def misfit(q):
        moved = image(q)
        return [right_side[c, q] - moved[c] for c in range(3)]

    def update(q, _):
        r0, r1, r2 = misfit(q)
        i00, i11, i22, i01, i02, i12 = [inverse[k, q] for k in range(6)]
        cur[0, q] += i00 * r0 + i01 * r1 + i02 * r2
        cur[1, q] += i01 * r0 + i11 * r1 + i12 * r2
        cur[2, q] += i02 * r0 + i12 * r1 + i22 * r2
        return forward(q, 0)

    def keep(q, _):
        for c, value in enumerate(misfit(q)):
            resid[c, q] = value
        return 0

    top = PAD + size_z
    arrived([(0, -1), (0, 1)])
    flat(pairs, pairs + own_pairs, stage_own)
    flat(PAD, top, forward)
    elements(PAD, top - 1, False)
    flat(PAD + 1, top - 1, invert, sum_modes(PAD))
    arrived([side for side in SIDES if side[0] != 0])
    flat(0, pairs, stage_halo)
    flat(pairs + own_pairs, 2 * pairs + own_pairs, stage_halo)
    flat(1, PAD, forward)
    flat(top, planes, forward)
    held = [[back[k, PAD, at] for at in tiles] for k in range(12)]
    elements(1, PAD, False)
    for k in range(12):
        for at, value in zip(tiles, held[k]):
            back[k, PAD, at] += value
    elements(top - 1, planes - 1, True)
    flat(2, PAD + 1, invert, sum_modes(1))
    flat(top - 1, planes - 1, invert, sum_modes(top - 2))
    flat(2, planes - 1, update)
    for sweep in range(1, SWEEPS):
        elements(sweep + 1, planes - 1 - sweep, False)
        flat(sweep + 2, planes - 1 - sweep, update)
    elements(PAD - 1, top + 1, False)
    flat(PAD, top + 1, keep)
    for c in range(3):
        for z in range(size_z):
            smooth[c, z] = cur[c, PAD + z, 0:size_y]

    seg_after_z = marked[0, 0:1, :]
    seg_after_y = marked[1, 0:1, :]
    maps = []
    for k in range(parts_z):
        want = slab * parts_z + k
        weights = []
        places = []
        for z in range(size_z):
            weights.append(jnp.where(seg_z[z] == want, 1.0, 0.0).astype(F32))
            places.append(0.5 * (slab * size_z + z - 4 * want - 2).astype(F32))
        count = sum(weights)
        moment = sum(w * p for w, p in zip(weights, places))
        last = jnp.where((seg_after_z == want.astype(F32)) & (slab < slabs - 1), 1.0, 0.0)
        place = 0.5 * ((slab + 1) * size_z - 4 * want - 2).astype(F32)
        weights.append(last)
        places.append(place)
        count = count + last
        centre = (moment + last * place) / count
        scale = lax.rsqrt(count)
        sums = [jnp.zeros((rows, width), F32) for _ in range(3)]
        turns = [jnp.zeros((rows, width), F32) for _ in range(2)]
        for z in range(size_z + 1):
            for c in range(3):
                part = weights[z] * resid[c, PAD + z]
                sums[c] = sums[c] + part
                if c < 2:
                    turns[c] = turns[c] + places[z] * part
        maps += [scale * s for s in sums]
        maps += [scale * (turns[c] - centre * sums[c]) for c in range(2)]

    lane = lax.broadcasted_iota(jnp.int32, (2 * parts_y, rows), 1)
    part = lax.broadcasted_iota(jnp.int32, (2 * parts_y, rows), 0)
    turned = part >= parts_y
    part = jnp.where(turned, part - parts_y, part) + sub * parts_y
    segments = jnp.full((2 * parts_y, rows), -1, jnp.int32)
    for y in range(size_y):
        segments = jnp.where(lane == y, seg_y[y], segments)
    after = jnp.broadcast_to(seg_after_y[:, :rows], segments.shape)
    hit = (lane == size_y) & (after == part.astype(F32)) & (sub < subs - 1)
    weight_y = jnp.where((segments == part) | hit, 1.0, 0.0)
    place_y = 0.5 * (lane + sub * size_y - 4 * part - 2).astype(F32)
    count = jnp.sum(weight_y, axis=1, keepdims=True)
    centre = jnp.sum(weight_y * place_y, axis=1, keepdims=True) / count
    weight_y = weight_y * lax.rsqrt(count) * jnp.where(turned, place_y - centre, 1.0)

    wide = jnp.concatenate(maps, axis=1)
    by_y = jnp.dot(
        weight_y, wide, precision=lax.Precision.HIGHEST, preferred_element_type=F32
    )
    tall = jnp.concatenate(
        [by_y[:, width * k : width * (k + 1)] for k in range(len(maps))], axis=0
    )
    by_x = lax.dot_general(
        tall,
        weights_x[...],
        (((1,), (1,)), ((), ())),
        precision=lax.Precision.HIGHEST,
        preferred_element_type=F32,
    )
    spread = parts_y * parts_x
    pick = lax.broadcasted_iota(jnp.int32, (parts_y, spread), 0) == (
        lax.broadcasted_iota(jnp.int32, (parts_y, spread), 1) // parts_x
    )

    def chosen(k, turn_y, turn_x):
        start = (2 * k + turn_y) * parts_y
        block = by_x[start : start + parts_y, turn_x * spread : (turn_x + 1) * spread]
        return jnp.sum(jnp.where(pick, block, 0.0), axis=0, keepdims=True)

    for k in range(parts_z):
        b = 5 * k
        values = [chosen(b, 0, 0), chosen(b + 1, 0, 0), chosen(b + 2, 0, 0)]
        values.append(chosen(b + 2, 1, 0) - chosen(b + 4, 0, 0))
        values.append(chosen(b + 3, 0, 0) - chosen(b + 2, 0, 1))
        values.append(chosen(b + 1, 0, 1) - chosen(b, 1, 0))
        for c in range(6):
            coarse[c, k : k + 1, :] = values[c]

    for dz, dy in SIDES:

        @pl.when(present(dz, dy))
        def _():
            for copy in copies[dz, dy]:
                copy.wait_send()


def on_device(field_init, load, modulus, seg_z, seg_y, seg_x):
    size_z, size_y, width = modulus.shape
    planes = size_z + 2 * PAD
    rows = size_y + 2 * PAD
    hbm = pl.BlockSpec(memory_space=pltpu.HBM)
    vmem = pl.BlockSpec(memory_space=pltpu.VMEM)
    block = (planes, rows, width)
    smooth, coarse = pl.pallas_call(
        functools.partial(kernel, unroll=UNROLL),
        out_shape=(
            jax.ShapeDtypeStruct((3, size_z, size_y, width), F32),
            jax.ShapeDtypeStruct((6, size_z // 4, size_y * width // 16), F32),
        ),
        in_specs=[hbm] * 6,
        out_specs=(vmem, vmem),
        scratch_shapes=[
            pltpu.SMEM(seg_z.shape, jnp.int32),
            pltpu.SMEM(seg_y.shape, jnp.int32),
            pltpu.VMEM((1, width), jnp.int32),
            pltpu.VMEM(field_init.shape, F32),
            pltpu.VMEM(load.shape, F32),
            pltpu.VMEM(modulus.shape, F32),
            pltpu.SemaphoreType.DMA((6,)),
            pltpu.VMEM((2, 7, size_z // 2, 8, width), F32),
            pltpu.VMEM((2, 7, planes // 2, 8, width), F32),
            pltpu.VMEM((7, planes, size_y, width), F32),
            pltpu.VMEM((2, 8, width), F32),
            pltpu.VMEM((2, 8, width), F32),
            pltpu.VMEM((size_y * width // 8, width), F32),
            pltpu.VMEM((3, *block), F32),
            pltpu.VMEM((3, *block), F32),
            pltpu.VMEM(block, F32),
            pltpu.VMEM((6, *block), F32),
            pltpu.VMEM((12, *block), F32),
            pltpu.VMEM((12, *block), F32),
            pltpu.VMEM((3, *block), F32),
            pltpu.SemaphoreType.DMA((len(SIDES), 4)),
            pltpu.SemaphoreType.DMA((len(SIDES), 4)),
        ],
        compiler_params=pltpu.CompilerParams(
            collective_id=0, has_side_effects=True, vmem_limit_bytes=(64 << 20) - (64 << 10)
        ),
        name="sweeps",
    )(seg_z, seg_y, seg_x.reshape(1, width), field_init, load, modulus)
    return smooth, coarse


def solution(mesh):
    in_specs = (
        P(None, "slab", "sub", None),
        P(None, "slab", "sub", None),
        P("slab", "sub", None),
        P("slab"),
        P("sub"),
        P(),
    )
    out_specs = (P(None, "slab", "sub", None), P(None, "slab", "sub"))
    return jax.shard_map(
        on_device, mesh=mesh, in_specs=in_specs, out_specs=out_specs, check_vma=False
    )
```

```python
import functools

import jax
import jax.numpy as jnp
from jax import lax
from jax.experimental import pallas as pl
from jax.experimental.pallas import tpu as pltpu
from jax.sharding import PartitionSpec as P

SWEEPS = 2
DAMPING = 0.6
PAD = 4
REACH = ((SWEEPS + 1, SWEEPS + 2), (SWEEPS, SWEEPS + 1), (SWEEPS + 1, SWEEPS + 1))
POISSON = 0.3
LAME = POISSON / ((1.0 + POISSON) * (1.0 - 2.0 * POISSON))
SHEAR = 0.5 / (1.0 + POISSON)
SIDES = ((-1, 0), (1, 0), (0, -1), (0, 1), (-1, -1), (-1, 1), (1, -1), (1, 1))
UNROLL = 2
MESH = pl.DeviceIdType.MESH
F32 = jnp.float32


def element_modes(lo, hi, e):
    def up(c, x, y):
        return lo[c][x][y] + hi[c][x][y]

    def diff(c, x, y):
        return hi[c][x][y] - lo[c][x][y]

    e_shear = e * (SHEAR / 16.0)
    e_shear2 = e * (SHEAR / 8.0)
    e_lame = e * (LAME / 16.0)
    e_lame3 = e * (LAME / 48.0)
    e_shear3 = e * (SHEAR / 48.0)
    e_last = e * ((LAME + 4.0 * SHEAR) / 144.0)
    out = [[[[None, None], [None, None]] for _ in range(2)] for _ in range(3)]

    n0, n1, n2 = up(0, 1, 0), up(1, 0, 1), diff(2, 0, 0)
    both = e_lame * (n0 + n1 + n2)
    out[0][1][0][0] = both + e_shear2 * n0
    out[1][0][1][0] = both + e_shear2 * n1
    out[2][0][0][1] = both + e_shear2 * n2

    both = e_shear * (up(0, 0, 1) + up(1, 1, 0))
    out[0][0][1][0] = both
    out[1][1][0][0] = both
    both = e_shear * (diff(0, 0, 0) + up(2, 1, 0))
    out[0][0][0][1] = both
    out[2][1][0][0] = both
    both = e_shear * (diff(1, 0, 0) + up(2, 0, 1))
    out[1][0][0][1] = both
    out[2][0][1][0] = both

    a, b = up(0, 1, 1), diff(2, 0, 1)
    both = e_lame3 * (a + b)
    out[0][1][1][0] = both + e_shear * a
    out[2][0][1][1] = both + e_shear * b
    a, b = diff(0, 1, 0), diff(1, 0, 1)
    both = e_lame3 * (a + b)
    out[0][1][0][1] = both + e_shear * a
    out[1][0][1][1] = both + e_shear * b
    a, b = up(1, 1, 1), diff(2, 1, 0)
    both = e_lame3 * (a + b)
    out[1][1][1][0] = both + e_shear * a
    out[2][1][0][1] = both + e_shear * b

    a, b, c = diff(0, 0, 1), diff(1, 1, 0), up(2, 1, 1)
    both = a + b + c
    out[0][0][1][1] = e_shear3 * (both + a)
    out[1][1][0][1] = e_shear3 * (both + b)
    out[2][1][1][0] = e_shear3 * (both + c)

    for c in range(3):
        out[c][1][1][1] = e_last * diff(c, 1, 1)
    return out


def flat(first, last, body, carry=0):
    for q in range(first, last):
        carry = body(q, carry)
    return carry


def kernel(
    seg_z_hbm,
    seg_y_hbm,
    seg_x_hbm,
    field_hbm,
    load_hbm,
    mod_hbm,
    smooth,
    coarse,
    seg_z,
    seg_y,
    seg_x,
    field,
    load,
    mod,
    own_sem,
    packed,
    tails,
    halo,
    mark,
    marked,
    weights_x,
    cur,
    right_side,
    emod,
    inverse,
    modes,
    back,
    resid,
    send_sem,
    recv_sem,
    *,
    unroll,
):
    size_z, size_y, width = smooth.shape[1:]
    planes, rows = cur.shape[1], cur.shape[2]
    slab, sub = lax.axis_index("slab"), lax.axis_index("sub")
    slabs, subs = lax.axis_size("slab"), lax.axis_size("sub")
    total_z, total_y = size_z * slabs, size_y * subs
    parts_z, parts_y, parts_x = size_z // 4, size_y // 4, width // 4
    pairs = PAD // 2
    own_pairs = size_z // 2

    def present(dz, dy):
        there = jnp.bool_(True)
        if dz == 1:
            there = there & (slab < slabs - 1)
        if dz == -1:
            there = there & (slab > 0)
        if dy == 1:
            there = there & (sub < subs - 1)
        if dy == -1:
            there = there & (sub > 0)
        return there

    barrier = pltpu.get_barrier_semaphore()
    for dz, dy in SIDES:

        @pl.when(present(dz, dy))
        def _():
            pl.semaphore_signal(
                barrier, inc=1, device_id=(slab + dz, sub + dy), device_id_type=MESH
            )

    own = [
        pltpu.make_async_copy(src, dst, own_sem.at[k])
        for k, (src, dst) in enumerate(
            (
                (field_hbm, field),
                (load_hbm, load),
                (mod_hbm, mod),
                (seg_z_hbm, seg_z),
                (seg_y_hbm, seg_y),
                (seg_x_hbm, seg_x),
            )
        )
    ]
    for copy in own:
        copy.start()
    for copy in own:
        copy.wait()

    first_half = lax.broadcasted_iota(jnp.int32, (8, width), 0) < PAD

    def unit(refs, k):
        return refs[k // 3].at[k % 3] if k < 6 else refs[2]

    inputs = (field, load, mod)

    def pack(i, _):
        for k in range(7):
            src = unit(inputs, k)
            a, b = src[2 * i, 0:8], src[2 * i + 1, 0:8]
            packed[0, k, i] = jnp.where(first_half, a, pltpu.roll(b, PAD, 0))
            a, b = src[2 * i, size_y - 8 : size_y], src[2 * i + 1, size_y - 8 : size_y]
            packed[1, k, i] = jnp.where(first_half, pltpu.roll(b, PAD, 0), a)
        return 0

    flat(0, own_pairs, pack)
    mark[0] = jnp.full((8, width), seg_z[0].astype(F32))
    mark[1] = jnp.full((8, width), seg_y[0].astype(F32))

    peers_z = 3 - (slab == 0).astype(jnp.int32) - (slab == slabs - 1).astype(jnp.int32)
    peers_y = 3 - (sub == 0).astype(jnp.int32) - (sub == subs - 1).astype(jnp.int32)
    pl.semaphore_wait(barrier, peers_z * peers_y - 1)

    copies = {}
    for side, (dz, dy) in enumerate(SIDES):
        group = []
        if dy == 0:
            for k, src in enumerate(inputs):
                low, high = REACH[k]
                if dz == 1:
                    start, to, count = size_z - low, PAD - low, low
                else:
                    start, to, count = 0, PAD + size_z, high
                if k < 2:
                    group.append(
                        (
                            src.at[:, pl.ds(start, count)],
                            halo.at[pl.ds(3 * k, 3), pl.ds(to, count)],
                        )
                    )
                else:
                    group.append((src.at[pl.ds(start, count)], halo.at[6, pl.ds(to, count)]))
        else:
            which = 0 if dy == -1 else 1
            start, to, count = {
                -1: (0, pairs + own_pairs, pairs),
                0: (0, pairs, own_pairs),
                1: (own_pairs - pairs, 0, pairs),
            }[dz]
            group.append(
                (
                    packed.at[which, :, pl.ds(start, count)],
                    tails.at[which, :, pl.ds(to, count)],
                )
            )
        if (dz, dy) == (-1, 0):
            group.append((mark.at[0], marked.at[0]))
        if (dz, dy) == (0, -1):
            group.append((mark.at[1], marked.at[1]))
        group = [
            pltpu.make_async_remote_copy(
                src_ref=from_ref,
                dst_ref=to_ref,
                send_sem=send_sem.at[side, k],
                recv_sem=recv_sem.at[side, k],
                device_id=(slab + dz, sub + dy),
                device_id_type=MESH,
            )
            for k, (from_ref, to_ref) in enumerate(group)
        ]
        copies[dz, dy] = group

        @pl.when(present(dz, dy))
        def _():
            for copy in group:
                copy.start()

    def arrived(sides):
        for dz, dy in sides:

            @pl.when(present(-dz, -dy))
            def _():
                for copy in copies[dz, dy]:
                    copy.wait_recv()

    square = (parts_y * parts_x, width)
    part = lax.rem(lax.broadcasted_iota(jnp.int32, square, 0), parts_x)
    weight_x = jnp.where(seg_x[...] == part, 1.0, 0.0)
    place_x = 0.5 * (lax.broadcasted_iota(jnp.int32, square, 1) - 4 * part - 2).astype(F32)
    count = jnp.sum(weight_x, axis=1, keepdims=True)
    centre = jnp.sum(weight_x * place_x, axis=1, keepdims=True) / count
    weight_x = weight_x * lax.rsqrt(count)
    weights_x[0 : square[0]] = weight_x
    weights_x[square[0] : 2 * square[0]] = weight_x * (place_x - centre)

    first_z = slab * size_z - PAD
    row = lax.broadcasted_iota(jnp.int32, (rows, width), 0)
    column = lax.broadcasted_iota(jnp.int32, (rows, width), 1)
    near = jnp.where(row < size_y + PAD, row, row - rows)
    glob_y = near + sub * size_y
    rows_in = (glob_y >= 0) & (glob_y < total_y)
    elements_in = (
        rows_in
        & (glob_y < total_y - 1)
        & (near >= -SWEEPS - 1)
        & (near < size_y + SWEEPS + 1)
        & (column < width - 1)
    )

    def left(v):
        return pltpu.roll(v, v.shape[1] - 1, 1)

    def right(v):
        return pltpu.roll(v, 1, 1)

    def lower(v):
        return pltpu.roll(v, v.shape[0] - 1, 0)

    def upper(v):
        return pltpu.roll(v, 1, 0)

    def stage(i, refs, shift):
        for k in range(7):
            src = unit(refs, k) if shift else halo.at[k]
            above, below = tails[0, k, i], tails[1, k, i]
            ends = (
                jnp.where(first_half, above, below),
                pltpu.roll(jnp.where(first_half, below, above), PAD, 0),
            )
            for odd in range(2):
                q = 2 * i + odd
                glob_z = q + first_z
                value = jnp.concatenate([src[q - shift], ends[odd]], axis=0)
                if k < 6:
                    keep = rows_in & (glob_z >= 0) & (glob_z < total_z)
                    value = jnp.where(keep, value, 0.0)
                    if k < 3:
                        cur[k, q] = value
                    else:
                        right_side[k - 3, q] = value
                else:
                    keep = elements_in & (glob_z >= 0) & (glob_z < total_z - 1)
                    emod[q] = jnp.where(keep, value, 0.0)

    def stage_own(i, _):
        stage(i, inputs, PAD)
        return 0

    def stage_halo(i, _):
        stage(i, None, 0)
        return 0

    def sum_modes(q):
        e = emod[q]
        r = right(e)
        s, d = e + r, r - e
        us, ud = upper(s), upper(d)
        return s + us, us - s, d + ud, ud - d

    def invert(q, before):
        now = sum_modes(q)
        main = (LAME + 4.0 * SHEAR) / 9.0
        side = (LAME + SHEAR) / 12.0
        p = main * (now[0] + before[0])
        xy = side * (now[3] + before[3])
        xz = side * (before[2] - now[2])
        yz = side * (before[1] - now[1])
        pp = p * p
        c00 = pp - yz * yz
        c11 = pp - xz * xz
        c22 = pp - xy * xy
        c01 = xz * yz - xy * p
        c02 = xy * yz - xz * p
        c12 = xy * xz - yz * p
        det = p * c00 + xy * c01 + xz * c02
        scale = DAMPING / jnp.where(p > 0.0, det, 1.0)
        for k, entry in enumerate((c00, c11, c22, c01, c02, c12)):
            inverse[k, q] = entry * scale
        return now

    def forward(q, sweep):
        for c in range(3):
            u = cur[c, q]
            a = left(u)
            for x, t in enumerate((u + a, a - u)):
                b = lower(t)
                modes[sweep, 4 * c + 2 * x, q] = t + b
                modes[sweep, 4 * c + 2 * x + 1, q] = b - t
        return sweep

    tiles = [pl.ds(8 * tile, 8) for tile in range(rows // 8)]

    def elements(sweep, first, last, begin, add):
        for at in tiles:

            def element(q, carry):
                lo = [
                    [[modes[sweep, 4 * c + 2 * x + y, q, at] for y in range(2)] for x in range(2)]
                    for c in range(3)
                ]
                hi = [
                    [
                        [modes[sweep, 4 * c + 2 * x + y, q + 1, at] for y in range(2)]
                        for x in range(2)
                    ]
                    for c in range(3)
                ]
                out = element_modes(lo, hi, emod[q, at])
                after = []
                for c in range(3):
                    for x in range(2):
                        for y in range(2):
                            k = 4 * c + 2 * x + y
                            total, change = out[c][x][y]
                            if total is None:
                                back[sweep, k, q, at] = carry[k] - change
                                after.append(change)
                            else:
                                back[sweep, k, q, at] = carry[k] + (total - change)
                                after.append(total + change)
                return tuple(after)

            if begin:
                carry = tuple(back[sweep, k, first, at] for k in range(12))
            else:
                carry = (jnp.zeros((8, width), F32),) * 12
            carry = lax.fori_loop(first, last, element, carry, unroll=unroll)
            for k in range(12):
                if add:
                    back[sweep, k, last, at] += carry[k]
                else:
                    back[sweep, k, last, at] = carry[k]

    def image(sweep, q):
        result = []
        for c in range(3):
            halves = []
            for x in range(2):
                k = 4 * c + 2 * x
                s, d = back[sweep, k, q], back[sweep, k + 1, q]
                halves.append((s - d) + upper(s + d))
            s, d = halves
            result.append((s - d) + right(s + d))
        return result

    def finish(q, sweep):
        moved = image(sweep, q)
        r0, r1, r2 = [right_side[c, q] - moved[c] for c in range(3)]
        if sweep == SWEEPS:
            for c, value in enumerate((r0, r1, r2)):
                resid[c, q] = value
            return sweep
        i00, i11, i22, i01, i02, i12 = [inverse[k, q] for k in range(6)]
        cur[0, q] += i00 * r0 + i01 * r1 + i02 * r2
        cur[1, q] += i01 * r0 + i11 * r1 + i12 * r2
        cur[2, q] += i02 * r0 + i12 * r1 + i22 * r2
        forward(q, sweep + 1)
        return sweep

    top = PAD + size_z
    arrived([(0, -1), (0, 1)])
    flat(pairs, pairs + own_pairs, stage_own)
    flat(PAD, top, forward)
    flat(PAD + 1, top - 1, invert, sum_modes(PAD))
    for sweep in range(SWEEPS + 1):
        first, last = PAD + sweep, top - 1 - sweep
        elements(sweep, first, last, False, False)
        flat(first + 1, last, finish, sweep)

    arrived([side for side in SIDES if side[0] != 0])
    flat(0, pairs, stage_halo)
    flat(pairs + own_pairs, 2 * pairs + own_pairs, stage_halo)
    flat(1, PAD, forward)
    flat(top, planes, forward)
    flat(2, PAD + 1, invert, sum_modes(1))
    flat(top - 1, planes - 1, invert, sum_modes(top - 2))
    for sweep in range(SWEEPS + 1):
        elements(sweep, 1 + sweep, PAD + sweep, False, True)
        elements(sweep, top - 1 - sweep, planes - 1 - sweep, True, False)
        flat(2 + sweep, PAD + sweep + 1, finish, sweep)
        flat(top - 1 - sweep, planes - 1 - sweep, finish, sweep)
    for c in range(3):
        for z in range(size_z):
            smooth[c, z] = cur[c, PAD + z, 0:size_y]

    seg_after_z = marked[0, 0:1, :]
    seg_after_y = marked[1, 0:1, :]
    maps = []
    for k in range(parts_z):
        want = slab * parts_z + k
        weights = []
        places = []
        for z in range(size_z):
            weights.append(jnp.where(seg_z[z] == want, 1.0, 0.0).astype(F32))
            places.append(0.5 * (slab * size_z + z - 4 * want - 2).astype(F32))
        count = sum(weights)
        moment = sum(w * p for w, p in zip(weights, places))
        last = jnp.where((seg_after_z == want.astype(F32)) & (slab < slabs - 1), 1.0, 0.0)
        place = 0.5 * ((slab + 1) * size_z - 4 * want - 2).astype(F32)
        weights.append(last)
        places.append(place)
        count = count + last
        centre = (moment + last * place) / count
        scale = lax.rsqrt(count)
        sums = [jnp.zeros((rows, width), F32) for _ in range(3)]
        turns = [jnp.zeros((rows, width), F32) for _ in range(2)]
        for z in range(size_z + 1):
            for c in range(3):
                part = weights[z] * resid[c, PAD + z]
                sums[c] = sums[c] + part
                if c < 2:
                    turns[c] = turns[c] + places[z] * part
        maps += [scale * s for s in sums]
        maps += [scale * (turns[c] - centre * sums[c]) for c in range(2)]

    lane = lax.broadcasted_iota(jnp.int32, (2 * parts_y, rows), 1)
    part = lax.broadcasted_iota(jnp.int32, (2 * parts_y, rows), 0)
    turned = part >= parts_y
    part = jnp.where(turned, part - parts_y, part) + sub * parts_y
    segments = jnp.full((2 * parts_y, rows), -1, jnp.int32)
    for y in range(size_y):
        segments = jnp.where(lane == y, seg_y[y], segments)
    after = jnp.broadcast_to(seg_after_y[:, :rows], segments.shape)
    hit = (lane == size_y) & (after == part.astype(F32)) & (sub < subs - 1)
    weight_y = jnp.where((segments == part) | hit, 1.0, 0.0)
    place_y = 0.5 * (lane + sub * size_y - 4 * part - 2).astype(F32)
    count = jnp.sum(weight_y, axis=1, keepdims=True)
    centre = jnp.sum(weight_y * place_y, axis=1, keepdims=True) / count
    weight_y = weight_y * lax.rsqrt(count) * jnp.where(turned, place_y - centre, 1.0)

    wide = jnp.concatenate(maps, axis=1)
    by_y = jnp.dot(
        weight_y, wide, precision=lax.Precision.HIGHEST, preferred_element_type=F32
    )
    tall = jnp.concatenate(
        [by_y[:, width * k : width * (k + 1)] for k in range(len(maps))], axis=0
    )
    by_x = lax.dot_general(
        tall,
        weights_x[...],
        (((1,), (1,)), ((), ())),
        precision=lax.Precision.HIGHEST,
        preferred_element_type=F32,
    )
    spread = parts_y * parts_x
    pick = lax.broadcasted_iota(jnp.int32, (parts_y, spread), 0) == (
        lax.broadcasted_iota(jnp.int32, (parts_y, spread), 1) // parts_x
    )

    def chosen(k, turn_y, turn_x):
        start = (2 * k + turn_y) * parts_y
        block = by_x[start : start + parts_y, turn_x * spread : (turn_x + 1) * spread]
        return jnp.sum(jnp.where(pick, block, 0.0), axis=0, keepdims=True)

    for k in range(parts_z):
        b = 5 * k
        values = [chosen(b, 0, 0), chosen(b + 1, 0, 0), chosen(b + 2, 0, 0)]
        values.append(chosen(b + 2, 1, 0) - chosen(b + 4, 0, 0))
        values.append(chosen(b + 3, 0, 0) - chosen(b + 2, 0, 1))
        values.append(chosen(b + 1, 0, 1) - chosen(b, 1, 0))
        for c in range(6):
            coarse[c, k : k + 1, :] = values[c]

    for dz, dy in SIDES:

        @pl.when(present(dz, dy))
        def _():
            for copy in copies[dz, dy]:
                copy.wait_send()


def on_device(field_init, load, modulus, seg_z, seg_y, seg_x):
    size_z, size_y, width = modulus.shape
    planes = size_z + 2 * PAD
    rows = size_y + 2 * PAD
    hbm = pl.BlockSpec(memory_space=pltpu.HBM)
    vmem = pl.BlockSpec(memory_space=pltpu.VMEM)
    block = (planes, rows, width)
    smooth, coarse = pl.pallas_call(
        functools.partial(kernel, unroll=UNROLL),
        out_shape=(
            jax.ShapeDtypeStruct((3, size_z, size_y, width), F32),
            jax.ShapeDtypeStruct((6, size_z // 4, size_y * width // 16), F32),
        ),
        in_specs=[hbm] * 6,
        out_specs=(vmem, vmem),
        scratch_shapes=[
            pltpu.SMEM(seg_z.shape, jnp.int32),
            pltpu.SMEM(seg_y.shape, jnp.int32),
            pltpu.VMEM((1, width), jnp.int32),
            pltpu.VMEM(field_init.shape, F32),
            pltpu.VMEM(load.shape, F32),
            pltpu.VMEM(modulus.shape, F32),
            pltpu.SemaphoreType.DMA((6,)),
            pltpu.VMEM((2, 7, size_z // 2, 8, width), F32),
            pltpu.VMEM((2, 7, planes // 2, 8, width), F32),
            pltpu.VMEM((7, planes, size_y, width), F32),
            pltpu.VMEM((2, 8, width), F32),
            pltpu.VMEM((2, 8, width), F32),
            pltpu.VMEM((size_y * width // 8, width), F32),
            pltpu.VMEM((3, *block), F32),
            pltpu.VMEM((3, *block), F32),
            pltpu.VMEM(block, F32),
            pltpu.VMEM((6, *block), F32),
            pltpu.VMEM((SWEEPS + 1, 12, *block), F32),
            pltpu.VMEM((SWEEPS + 1, 12, *block), F32),
            pltpu.VMEM((3, *block), F32),
            pltpu.SemaphoreType.DMA((len(SIDES), 4)),
            pltpu.SemaphoreType.DMA((len(SIDES), 4)),
        ],
        compiler_params=pltpu.CompilerParams(
            collective_id=0, has_side_effects=True, vmem_limit_bytes=(64 << 20) - (64 << 10)
        ),
        name="sweeps",
    )(seg_z, seg_y, seg_x.reshape(1, width), field_init, load, modulus)
    return smooth, coarse


def solution(mesh):
    in_specs = (
        P(None, "slab", "sub", None),
        P(None, "slab", "sub", None),
        P("slab", "sub", None),
        P("slab"),
        P("sub"),
        P(),
    )
    out_specs = (P(None, "slab", "sub", None), P(None, "slab", "sub"))
    return jax.shard_map(
        on_device, mesh=mesh, in_specs=in_specs, out_specs=out_specs, check_vma=False
    )
```

```python
import functools

import jax
import jax.numpy as jnp
from jax import lax
from jax.experimental import pallas as pl
from jax.experimental.pallas import tpu as pltpu
from jax.sharding import PartitionSpec as P

SWEEPS = 2
DAMPING = 0.6
PAD = 4
REACH = ((SWEEPS + 1, SWEEPS + 2), (SWEEPS, SWEEPS + 1), (SWEEPS + 1, SWEEPS + 1))
POISSON = 0.3
LAME = POISSON / ((1.0 + POISSON) * (1.0 - 2.0 * POISSON))
SHEAR = 0.5 / (1.0 + POISSON)
SIDES = ((0, -1), (0, 1), (-1, 0), (1, 0), (-1, -1), (1, 1), (-1, 1), (1, -1))
UNROLL = 2
MESH = pl.DeviceIdType.MESH
F32 = jnp.float32
BF16 = jnp.bfloat16


def element_modes(lo, hi, e):
    def up(c, x, y):
        return lo[c][x][y] + hi[c][x][y]

    def diff(c, x, y):
        return hi[c][x][y] - lo[c][x][y]

    e_shear = e * (SHEAR / 16.0)
    e_shear2 = e * (SHEAR / 8.0)
    e_lame = e * (LAME / 16.0)
    e_lame3 = e * (LAME / 48.0)
    e_shear3 = e * (SHEAR / 48.0)
    e_last = e * ((LAME + 4.0 * SHEAR) / 144.0)
    out = [[[[None, None], [None, None]] for _ in range(2)] for _ in range(3)]

    n0, n1, n2 = up(0, 1, 0), up(1, 0, 1), diff(2, 0, 0)
    both = e_lame * (n0 + n1 + n2)
    out[0][1][0][0] = both + e_shear2 * n0
    out[1][0][1][0] = both + e_shear2 * n1
    out[2][0][0][1] = both + e_shear2 * n2

    both = e_shear * (up(0, 0, 1) + up(1, 1, 0))
    out[0][0][1][0] = both
    out[1][1][0][0] = both
    both = e_shear * (diff(0, 0, 0) + up(2, 1, 0))
    out[0][0][0][1] = both
    out[2][1][0][0] = both
    both = e_shear * (diff(1, 0, 0) + up(2, 0, 1))
    out[1][0][0][1] = both
    out[2][0][1][0] = both

    a, b = up(0, 1, 1), diff(2, 0, 1)
    both = e_lame3 * (a + b)
    out[0][1][1][0] = both + e_shear * a
    out[2][0][1][1] = both + e_shear * b
    a, b = diff(0, 1, 0), diff(1, 0, 1)
    both = e_lame3 * (a + b)
    out[0][1][0][1] = both + e_shear * a
    out[1][0][1][1] = both + e_shear * b
    a, b = up(1, 1, 1), diff(2, 1, 0)
    both = e_lame3 * (a + b)
    out[1][1][1][0] = both + e_shear * a
    out[2][1][0][1] = both + e_shear * b

    a, b, c = diff(0, 0, 1), diff(1, 1, 0), up(2, 1, 1)
    both = a + b + c
    out[0][0][1][1] = e_shear3 * (both + a)
    out[1][1][0][1] = e_shear3 * (both + b)
    out[2][1][1][0] = e_shear3 * (both + c)

    for c in range(3):
        out[c][1][1][1] = e_last * diff(c, 1, 1)
    return out


def corner_planes(dz, size_z):
    held = []
    for k in range(7):
        low, high = REACH[k // 3]
        if dz == 1:
            held += [(k, size_z - low + i, PAD - low + i) for i in range(low)]
        else:
            held += [(k, i, PAD + size_z + i) for i in range(high)]
    return held


def two_parts(v):
    high = v.astype(BF16)
    return high, (v - high.astype(F32)).astype(BF16)


def flat(first, last, body, carry=0):
    for q in range(first, last):
        carry = body(q, carry)
    return carry


def kernel(
    seg_z_hbm,
    seg_y_hbm,
    seg_x_hbm,
    field_hbm,
    load_hbm,
    mod_hbm,
    smooth,
    coarse,
    seg_z,
    seg_y,
    seg_x,
    field,
    load,
    mod,
    own_sem,
    result_sem,
    packed,
    tails,
    corners,
    corner_tails,
    halo,
    mark,
    marked,
    weights_x,
    cur,
    right_side,
    emod,
    inverse,
    modes,
    back,
    resid,
    send_sem,
    recv_sem,
    *,
    unroll,
):
    size_z, size_y, width = smooth.shape[1:]
    planes, rows = cur.shape[1], cur.shape[2]
    slab, sub = lax.axis_index("slab"), lax.axis_index("sub")
    slabs, subs = lax.axis_size("slab"), lax.axis_size("sub")
    total_z, total_y = size_z * slabs, size_y * subs
    parts_z, parts_y, parts_x = size_z // 4, size_y // 4, width // 4
    own_pairs = size_z // 2

    def present(dz, dy):
        there = jnp.bool_(True)
        if dz == 1:
            there = there & (slab < slabs - 1)
        if dz == -1:
            there = there & (slab > 0)
        if dy == 1:
            there = there & (sub < subs - 1)
        if dy == -1:
            there = there & (sub > 0)
        return there

    barrier = pltpu.get_barrier_semaphore()
    for dz, dy in SIDES:

        @pl.when(present(dz, dy))
        def _():
            pl.semaphore_signal(
                barrier, inc=1, device_id=(slab + dz, sub + dy), device_id_type=MESH
            )

    own = [
        pltpu.make_async_copy(src, dst, own_sem.at[k])
        for k, (src, dst) in enumerate(
            (
                (field_hbm, field),
                (load_hbm, load),
                (mod_hbm, mod),
                (seg_z_hbm, seg_z),
                (seg_y_hbm, seg_y),
                (seg_x_hbm, seg_x),
            )
        )
    ]
    for copy in own:
        copy.start()
    for copy in own:
        copy.wait()

    first_half = lax.broadcasted_iota(jnp.int32, (8, width), 0) < PAD

    def unit(refs, k):
        return refs[k // 3].at[k % 3] if k < 6 else refs[2]

    inputs = (field, load, mod)

    def pack(i, _):
        for k in range(7):
            src = unit(inputs, k)
            a, b = src[2 * i, 0:8], src[2 * i + 1, 0:8]
            packed[0, k, i] = jnp.where(first_half, a, pltpu.roll(b, PAD, 0))
            a, b = src[2 * i, size_y - 8 : size_y], src[2 * i + 1, size_y - 8 : size_y]
            packed[1, k, i] = jnp.where(first_half, pltpu.roll(b, PAD, 0), a)
        return 0

    flat(0, own_pairs, pack)
    for dz in (-1, 1):
        held = corner_planes(dz, size_z)
        for n in range(0, len(held), 2):
            (ka, za, _), (kb, zb, _) = held[n], held[min(n + 1, len(held) - 1)]
            a, b = unit(inputs, ka), unit(inputs, kb)
            corners[0, (dz + 1) // 2, n // 2] = jnp.where(
                first_half, a[za, 0:8], pltpu.roll(b[zb, 0:8], PAD, 0)
            )
            corners[1, (dz + 1) // 2, n // 2] = jnp.where(
                first_half,
                pltpu.roll(b[zb, size_y - 8 : size_y], PAD, 0),
                a[za, size_y - 8 : size_y],
            )
    mark[0] = jnp.full((8, width), seg_z[0].astype(F32))
    mark[1] = jnp.full((8, width), seg_y[0].astype(F32))

    peers_z = 3 - (slab == 0).astype(jnp.int32) - (slab == slabs - 1).astype(jnp.int32)
    peers_y = 3 - (sub == 0).astype(jnp.int32) - (sub == subs - 1).astype(jnp.int32)
    pl.semaphore_wait(barrier, peers_z * peers_y - 1)

    copies = {}
    for side, (dz, dy) in enumerate(SIDES):
        group = []
        if dy == 0:
            for k, src in enumerate(inputs):
                low, high = REACH[k]
                if dz == 1:
                    start, to, count = size_z - low, PAD - low, low
                else:
                    start, to, count = 0, PAD + size_z, high
                if k < 2:
                    group.append(
                        (
                            src.at[:, pl.ds(start, count)],
                            halo.at[pl.ds(3 * k, 3), pl.ds(to, count)],
                        )
                    )
                else:
                    group.append((src.at[pl.ds(start, count)], halo.at[6, pl.ds(to, count)]))
        else:
            which = 0 if dy == -1 else 1
            if dz == 0:
                group.append((packed.at[which], tails.at[which]))
            else:
                tall = pl.ds(0, (len(corner_planes(dz, size_z)) + 1) // 2)
                at = (which, (dz + 1) // 2, tall)
                group.append((corners.at[at], corner_tails.at[at]))
        if (dz, dy) == (-1, 0):
            group.append((mark.at[0], marked.at[0]))
        if (dz, dy) == (0, -1):
            group.append((mark.at[1], marked.at[1]))
        group = [
            pltpu.make_async_remote_copy(
                src_ref=from_ref,
                dst_ref=to_ref,
                send_sem=send_sem.at[side, k],
                recv_sem=recv_sem.at[side, k],
                device_id=(slab + dz, sub + dy),
                device_id_type=MESH,
            )
            for k, (from_ref, to_ref) in enumerate(group)
        ]
        copies[dz, dy] = group

        @pl.when(present(dz, dy))
        def _():
            for copy in group:
                copy.start()

    def arrived(sides):
        for dz, dy in sides:

            @pl.when(present(-dz, -dy))
            def _():
                for copy in copies[dz, dy]:
                    copy.wait_recv()

    square = (parts_y * parts_x, width)
    part = lax.rem(lax.broadcasted_iota(jnp.int32, square, 0), parts_x)
    weight_x = jnp.where(seg_x[...] == part, 1.0, 0.0)
    place_x = 0.5 * (lax.broadcasted_iota(jnp.int32, square, 1) - 4 * part - 2).astype(F32)
    weight_x = jnp.concatenate([weight_x, weight_x * place_x], axis=0).astype(BF16)
    weights_x[:, 0:width] = weight_x
    weights_x[:, width : 2 * width] = weight_x
    alone = lax.dot_general(
        jnp.ones((16, width), BF16),
        weight_x,
        (((1,), (1,)), ((), ())),
        preferred_element_type=F32,
    )
    spread = square[0]
    count_x, moment_x = alone[0:1, 0:spread], alone[0:1, spread : 2 * spread]

    first_z = slab * size_z - PAD
    row = lax.broadcasted_iota(jnp.int32, (rows, width), 0)
    column = lax.broadcasted_iota(jnp.int32, (rows, width), 1)
    near = jnp.where(row < size_y + PAD, row, row - rows)
    glob_y = near + sub * size_y
    rows_in = (glob_y >= 0) & (glob_y < total_y)
    elements_in = (
        rows_in
        & (glob_y < total_y - 1)
        & (near >= -SWEEPS - 1)
        & (near < size_y + SWEEPS + 1)
        & (column < width - 1)
    )

    def left(v):
        return pltpu.roll(v, v.shape[1] - 1, 1)

    def right(v):
        return pltpu.roll(v, 1, 1)

    def lower(v):
        return pltpu.roll(v, v.shape[0] - 1, 0)

    def upper(v):
        return pltpu.roll(v, 1, 0)

    def place(k, q, main, above, below, odd):
        if odd:
            end = pltpu.roll(jnp.where(first_half, below, above), PAD, 0)
        else:
            end = jnp.where(first_half, above, below)
        value = jnp.concatenate([main, end], axis=0)
        glob_z = q + first_z
        if k < 6:
            keep = rows_in & (glob_z >= 0) & (glob_z < total_z)
            value = jnp.where(keep, value, 0.0)
            if k < 3:
                cur[k, q] = value
            else:
                right_side[k - 3, q] = value
        else:
            keep = elements_in & (glob_z >= 0) & (glob_z < total_z - 1)
            emod[q] = jnp.where(keep, value, 0.0)

    def stage_own(i, _):
        for k in range(7):
            src = unit(inputs, k)
            for odd in range(2):
                z = 2 * i + odd
                place(k, z + PAD, src[z], tails[0, k, i], tails[1, k, i], odd)
        return 0

    def stage_halo(dz):
        side = (dz + 1) // 2
        for n, (k, _, q) in enumerate(corner_planes(dz, size_z)):
            above, below = corner_tails[0, side, n // 2], corner_tails[1, side, n // 2]
            place(k, q, halo[k, q], above, below, n % 2)

    def sum_modes(q):
        e = emod[q]
        r = right(e)
        s, d = e + r, r - e
        us, ud = upper(s), upper(d)
        return s + us, us - s, d + ud, ud - d

    def invert(q, before):
        now = sum_modes(q)
        main = (LAME + 4.0 * SHEAR) / 9.0
        side = (LAME + SHEAR) / 12.0
        p = main * (now[0] + before[0])
        xy = side * (now[3] + before[3])
        xz = side * (before[2] - now[2])
        yz = side * (before[1] - now[1])
        pp = p * p
        c00 = pp - yz * yz
        c11 = pp - xz * xz
        c22 = pp - xy * xy
        c01 = xz * yz - xy * p
        c02 = xy * yz - xz * p
        c12 = xy * xz - yz * p
        det = p * c00 + xy * c01 + xz * c02
        scale = DAMPING / jnp.where(p > 0.0, det, 1.0)
        for k, entry in enumerate((c00, c11, c22, c01, c02, c12)):
            inverse[k, q] = entry * scale
        return now

    def forward(q, sweep):
        for c in range(3):
            u = cur[c, q]
            a = left(u)
            for x, t in enumerate((u + a, a - u)):
                b = lower(t)
                modes[sweep, 4 * c + 2 * x, q] = t + b
                modes[sweep, 4 * c + 2 * x + 1, q] = b - t
        return sweep

    tiles = [pl.ds(8 * tile, 8) for tile in range(rows // 8)]

    def elements(sweep, first, last, begin, add):
        for at in tiles:

            def element(q, carry):
                lo = [
                    [[modes[sweep, 4 * c + 2 * x + y, q, at] for y in range(2)] for x in range(2)]
                    for c in range(3)
                ]
                hi = [
                    [
                        [modes[sweep, 4 * c + 2 * x + y, q + 1, at] for y in range(2)]
                        for x in range(2)
                    ]
                    for c in range(3)
                ]
                out = element_modes(lo, hi, emod[q, at])
                after = []
                for c in range(3):
                    for x in range(2):
                        for y in range(2):
                            k = 4 * c + 2 * x + y
                            total, change = out[c][x][y]
                            if total is None:
                                back[sweep, k, q, at] = carry[k] - change
                                after.append(change)
                            else:
                                back[sweep, k, q, at] = carry[k] + (total - change)
                                after.append(total + change)
                return tuple(after)

            if begin:
                carry = tuple(back[sweep, k, first, at] for k in range(12))
            else:
                carry = (jnp.zeros((8, width), F32),) * 12
            carry = lax.fori_loop(first, last, element, carry, unroll=unroll)
            for k in range(12):
                if add:
                    back[sweep, k, last, at] += carry[k]
                else:
                    back[sweep, k, last, at] = carry[k]

    def image(sweep, q):
        result = []
        for c in range(3):
            halves = []
            for x in range(2):
                k = 4 * c + 2 * x
                s, d = back[sweep, k, q], back[sweep, k + 1, q]
                halves.append((s - d) + upper(s + d))
            s, d = halves
            result.append((s - d) + right(s + d))
        return result

    def finish(q, sweep):
        moved = image(sweep, q)
        r0, r1, r2 = [right_side[c, q] - moved[c] for c in range(3)]
        if sweep == SWEEPS:
            for c, value in enumerate((r0, r1, r2)):
                resid[c, q] = value
            return sweep
        i00, i11, i22, i01, i02, i12 = [inverse[k, q] for k in range(6)]
        cur[0, q] += i00 * r0 + i01 * r1 + i02 * r2
        cur[1, q] += i01 * r0 + i11 * r1 + i12 * r2
        cur[2, q] += i02 * r0 + i12 * r1 + i22 * r2
        forward(q, sweep + 1)
        return sweep

    top = PAD + size_z
    arrived([(0, -1), (0, 1)])
    flat(0, own_pairs, stage_own)
    flat(PAD, top, forward)
    flat(PAD + 1, top - 1, invert, sum_modes(PAD))
    for sweep in range(SWEEPS + 1):
        first, last = PAD + sweep, top - 1 - sweep
        elements(sweep, first, last, False, False)
        flat(first + 1, last, finish, sweep)

    arrived([side for side in SIDES if side[0] != 0])
    stage_halo(1)
    stage_halo(-1)
    flat(1, PAD, forward)
    flat(top, planes, forward)
    flat(2, PAD + 1, invert, sum_modes(1))
    flat(top - 1, planes - 1, invert, sum_modes(top - 2))
    result = pltpu.make_async_copy(
        cur.at[:, pl.ds(PAD, size_z), pl.ds(0, size_y)], smooth, result_sem
    )
    for sweep in range(SWEEPS + 1):
        if sweep == SWEEPS:
            result.start()
        elements(sweep, 1 + sweep, PAD + sweep, False, True)
        elements(sweep, top - 1 - sweep, planes - 1 - sweep, True, False)
        flat(2 + sweep, PAD + sweep + 1, finish, sweep)
        flat(top - 1 - sweep, planes - 1 - sweep, finish, sweep)
    seg_after_z = marked[0, 0:1, :]
    seg_after_y = marked[1, 0:1, :]
    maps = []
    along_z = []
    for k in range(parts_z):
        want = slab * parts_z + k
        weights = []
        places = []
        for z in range(size_z):
            weights.append(jnp.where(seg_z[z] == want, 1.0, 0.0).astype(F32))
            places.append(0.5 * (slab * size_z + z - 4 * want - 2).astype(F32))
        last = jnp.where((seg_after_z == want.astype(F32)) & (slab < slabs - 1), 1.0, 0.0)
        weights.append(last)
        places.append(0.5 * ((slab + 1) * size_z - 4 * want - 2).astype(F32))
        along_z.append((sum(weights), sum(w * p for w, p in zip(weights, places))))
        sums = [jnp.zeros((rows, width), F32) for _ in range(3)]
        turns = [jnp.zeros((rows, width), F32) for _ in range(2)]
        for z in range(size_z + 1):
            for c in range(3):
                part = weights[z] * resid[c, PAD + z]
                sums[c] = sums[c] + part
                if c < 2:
                    turns[c] = turns[c] + places[z] * part
        maps += sums + turns

    lane = lax.broadcasted_iota(jnp.int32, (2 * parts_y, rows), 1)
    part = lax.broadcasted_iota(jnp.int32, (2 * parts_y, rows), 0)
    turned = part >= parts_y
    part = jnp.where(turned, part - parts_y, part) + sub * parts_y
    segments = jnp.full((2 * parts_y, rows), -1, jnp.int32)
    for y in range(size_y):
        segments = jnp.where(lane == y, seg_y[y], segments)
    after = jnp.broadcast_to(seg_after_y[:, :rows], segments.shape)
    hit = (lane == size_y) & (after == part.astype(F32)) & (sub < subs - 1)
    weight_y = jnp.where((segments == part) | hit, 1.0, 0.0)
    place_y = 0.5 * (lane + sub * size_y - 4 * part - 2).astype(F32)
    weight_y = weight_y * jnp.where(turned, place_y, 1.0)
    along_y = jnp.sum(weight_y, axis=1, keepdims=True)

    high, low = two_parts(jnp.concatenate(maps, axis=1))
    weight_y = weight_y.astype(BF16)
    by_y = jnp.dot(weight_y, high, preferred_element_type=F32)
    by_y = by_y + jnp.dot(weight_y, low, preferred_element_type=F32)
    tall = jnp.concatenate(
        [by_y[:, width * k : width * (k + 1)] for k in range(len(maps))], axis=0
    )
    by_x = lax.dot_general(
        jnp.concatenate(two_parts(tall), axis=1),
        weights_x[...],
        (((1,), (1,)), ((), ())),
        preferred_element_type=F32,
    )
    pick = lax.broadcasted_iota(jnp.int32, (parts_y, spread), 0) == (
        lax.broadcasted_iota(jnp.int32, (parts_y, spread), 1) // parts_x
    )

    def picked(block):
        return jnp.sum(jnp.where(pick, block, 0.0), axis=0, keepdims=True)

    def chosen(k, turn_y, turn_x):
        start = (2 * k + turn_y) * parts_y
        return picked(by_x[start : start + parts_y, turn_x * spread : (turn_x + 1) * spread])

    count_y, moment_y = picked(along_y[0:parts_y]), picked(along_y[parts_y : 2 * parts_y])
    for k in range(parts_z):
        b = 5 * k
        count_z, moment_z = along_z[k]
        centre_x, centre_y, centre_z = moment_x / count_x, moment_y / count_y, moment_z / count_z
        scale = lax.rsqrt(count_x * count_y * count_z)
        s0, s1, s2 = chosen(b, 0, 0), chosen(b + 1, 0, 0), chosen(b + 2, 0, 0)
        t0 = chosen(b + 2, 1, 0) - chosen(b + 4, 0, 0) - (centre_y * s2 - centre_z * s1)
        t1 = chosen(b + 3, 0, 0) - chosen(b + 2, 0, 1) - (centre_z * s0 - centre_x * s2)
        t2 = chosen(b + 1, 0, 1) - chosen(b, 1, 0) - (centre_x * s1 - centre_y * s0)
        for c, value in enumerate((s0, s1, s2, t0, t1, t2)):
            coarse[c, k : k + 1, :] = value * scale

    for dz, dy in SIDES:

        @pl.when(present(dz, dy))
        def _():
            for copy in copies[dz, dy]:
                copy.wait_send()

    result.wait()


def on_device(field_init, load, modulus, seg_z, seg_y, seg_x):
    size_z, size_y, width = modulus.shape
    planes = size_z + 2 * PAD
    rows = size_y + 2 * PAD
    hbm = pl.BlockSpec(memory_space=pltpu.HBM)
    vmem = pl.BlockSpec(memory_space=pltpu.VMEM)
    block = (planes, rows, width)
    corner_tiles = max((len(corner_planes(dz, size_z)) + 1) // 2 for dz in (-1, 1))
    smooth, coarse = pl.pallas_call(
        functools.partial(kernel, unroll=UNROLL),
        out_shape=(
            jax.ShapeDtypeStruct((3, size_z, size_y, width), F32),
            jax.ShapeDtypeStruct((6, size_z // 4, size_y * width // 16), F32),
        ),
        in_specs=[hbm] * 6,
        out_specs=(hbm, vmem),
        scratch_shapes=[
            pltpu.SMEM(seg_z.shape, jnp.int32),
            pltpu.SMEM(seg_y.shape, jnp.int32),
            pltpu.VMEM((1, width), jnp.int32),
            pltpu.VMEM(field_init.shape, F32),
            pltpu.VMEM(load.shape, F32),
            pltpu.VMEM(modulus.shape, F32),
            pltpu.SemaphoreType.DMA((6,)),
            pltpu.SemaphoreType.DMA,
            pltpu.VMEM((2, 7, size_z // 2, 8, width), F32),
            pltpu.VMEM((2, 7, size_z // 2, 8, width), F32),
            pltpu.VMEM((2, 2, corner_tiles, 8, width), F32),
            pltpu.VMEM((2, 2, corner_tiles, 8, width), F32),
            pltpu.VMEM((7, planes, size_y, width), F32),
            pltpu.VMEM((2, 8, width), F32),
            pltpu.VMEM((2, 8, width), F32),
            pltpu.VMEM((size_y * width // 8, 2 * width), BF16),
            pltpu.VMEM((3, *block), F32),
            pltpu.VMEM((3, *block), F32),
            pltpu.VMEM(block, F32),
            pltpu.VMEM((6, *block), F32),
            pltpu.VMEM((SWEEPS + 1, 12, *block), F32),
            pltpu.VMEM((SWEEPS + 1, 12, *block), F32),
            pltpu.VMEM((3, *block), F32),
            pltpu.SemaphoreType.DMA((len(SIDES), 4)),
            pltpu.SemaphoreType.DMA((len(SIDES), 4)),
        ],
        compiler_params=pltpu.CompilerParams(
            collective_id=0, has_side_effects=True, vmem_limit_bytes=(64 << 20) - (64 << 10)
        ),
        name="sweeps",
    )(seg_z, seg_y, seg_x.reshape(1, width), field_init, load, modulus)
    return smooth, coarse


def solution(mesh):
    in_specs = (
        P(None, "slab", "sub", None),
        P(None, "slab", "sub", None),
        P("slab", "sub", None),
        P("slab"),
        P("sub"),
        P(),
    )
    out_specs = (P(None, "slab", "sub", None), P(None, "slab", "sub"))
    return jax.shard_map(
        on_device, mesh=mesh, in_specs=in_specs, out_specs=out_specs, check_vma=False
    )
```

```python
import functools

import jax
import jax.numpy as jnp
from jax import lax
from jax.experimental import pallas as pl
from jax.experimental.pallas import tpu as pltpu
from jax.sharding import PartitionSpec as P

SWEEPS = 2
DAMPING = 0.6
PAD = 4
REACH = ((SWEEPS + 1, SWEEPS + 2), (SWEEPS, SWEEPS + 1), (SWEEPS + 1, SWEEPS + 1))
POISSON = 0.3
LAME = POISSON / ((1.0 + POISSON) * (1.0 - 2.0 * POISSON))
SHEAR = 0.5 / (1.0 + POISSON)
SIDES = ((0, -1), (0, 1), (-1, 0), (1, 0), (-1, -1), (1, 1), (-1, 1), (1, -1))
UNROLL = 2
MESH = pl.DeviceIdType.MESH
F32 = jnp.float32
BF16 = jnp.bfloat16


def element_modes(lo, hi, e):
    def up(c, x, y):
        return lo[c][x][y] + hi[c][x][y]

    def diff(c, x, y):
        return hi[c][x][y] - lo[c][x][y]

    e_shear = e * (SHEAR / 16.0)
    e_shear2 = e * (SHEAR / 8.0)
    e_lame = e * (LAME / 16.0)
    e_lame3 = e * (LAME / 48.0)
    e_shear3 = e * (SHEAR / 48.0)
    e_last = e * ((LAME + 4.0 * SHEAR) / 144.0)
    out = [[[[None, None], [None, None]] for _ in range(2)] for _ in range(3)]

    n0, n1, n2 = up(0, 1, 0), up(1, 0, 1), diff(2, 0, 0)
    both = e_lame * (n0 + n1 + n2)
    out[0][1][0][0] = both + e_shear2 * n0
    out[1][0][1][0] = both + e_shear2 * n1
    out[2][0][0][1] = both + e_shear2 * n2

    both = e_shear * (up(0, 0, 1) + up(1, 1, 0))
    out[0][0][1][0] = both
    out[1][1][0][0] = both
    both = e_shear * (diff(0, 0, 0) + up(2, 1, 0))
    out[0][0][0][1] = both
    out[2][1][0][0] = both
    both = e_shear * (diff(1, 0, 0) + up(2, 0, 1))
    out[1][0][0][1] = both
    out[2][0][1][0] = both

    a, b = up(0, 1, 1), diff(2, 0, 1)
    both = e_lame3 * (a + b)
    out[0][1][1][0] = both + e_shear * a
    out[2][0][1][1] = both + e_shear * b
    a, b = diff(0, 1, 0), diff(1, 0, 1)
    both = e_lame3 * (a + b)
    out[0][1][0][1] = both + e_shear * a
    out[1][0][1][1] = both + e_shear * b
    a, b = up(1, 1, 1), diff(2, 1, 0)
    both = e_lame3 * (a + b)
    out[1][1][1][0] = both + e_shear * a
    out[2][1][0][1] = both + e_shear * b

    a, b, c = diff(0, 0, 1), diff(1, 1, 0), up(2, 1, 1)
    both = a + b + c
    out[0][0][1][1] = e_shear3 * (both + a)
    out[1][1][0][1] = e_shear3 * (both + b)
    out[2][1][1][0] = e_shear3 * (both + c)

    for c in range(3):
        out[c][1][1][1] = e_last * diff(c, 1, 1)
    return out


def corner_planes(dz, size_z):
    held = []
    for k in range(7):
        low, high = REACH[k // 3]
        if dz == 1:
            held += [(k, size_z - low + i, PAD - low + i) for i in range(low)]
        else:
            held += [(k, i, PAD + size_z + i) for i in range(high)]
    return held


def two_parts(v):
    high = v.astype(BF16)
    return high, (v - high.astype(F32)).astype(BF16)


def flat(first, last, body, carry=0):
    for q in range(first, last):
        carry = body(q, carry)
    return carry


def kernel(
    seg_z_hbm,
    seg_y_hbm,
    seg_x_hbm,
    field_hbm,
    load_hbm,
    mod_hbm,
    smooth,
    coarse,
    seg_z,
    seg_y,
    seg_x,
    field,
    load,
    mod,
    own_sem,
    result_sem,
    packed,
    tails,
    corners,
    corner_tails,
    halo,
    mark,
    marked,
    weights_x,
    cur,
    right_side,
    emod,
    inverse,
    modes,
    back,
    resid,
    send_sem,
    recv_sem,
    *,
    unroll,
):
    size_z, size_y, width = smooth.shape[1:]
    planes, rows = cur.shape[1], cur.shape[2]
    slab, sub = lax.axis_index("slab"), lax.axis_index("sub")
    slabs, subs = lax.axis_size("slab"), lax.axis_size("sub")
    total_z, total_y = size_z * slabs, size_y * subs
    parts_z, parts_y, parts_x = size_z // 4, size_y // 4, width // 4
    own_pairs = size_z // 2

    def present(dz, dy):
        there = jnp.bool_(True)
        if dz == 1:
            there = there & (slab < slabs - 1)
        if dz == -1:
            there = there & (slab > 0)
        if dy == 1:
            there = there & (sub < subs - 1)
        if dy == -1:
            there = there & (sub > 0)
        return there

    barrier = pltpu.get_barrier_semaphore()
    for dz, dy in SIDES:

        @pl.when(present(dz, dy))
        def _():
            pl.semaphore_signal(
                barrier, inc=1, device_id=(slab + dz, sub + dy), device_id_type=MESH
            )

    own = [
        pltpu.make_async_copy(src, dst, own_sem.at[k])
        for k, (src, dst) in enumerate(
            (
                (field_hbm, field),
                (load_hbm, load),
                (mod_hbm, mod),
                (seg_z_hbm, seg_z),
                (seg_y_hbm, seg_y),
                (seg_x_hbm, seg_x),
            )
        )
    ]
    for copy in own:
        copy.start()
    for copy in own:
        copy.wait()

    first_half = lax.broadcasted_iota(jnp.int32, (8, width), 0) < PAD

    def unit(refs, k):
        return refs[k // 3].at[k % 3] if k < 6 else refs[2]

    inputs = (field, load, mod)

    def pack(i, _):
        for k in range(7):
            src = unit(inputs, k)
            a, b = src[2 * i, 0:8], src[2 * i + 1, 0:8]
            packed[0, k, i] = jnp.where(first_half, a, pltpu.roll(b, PAD, 0))
            a, b = src[2 * i, size_y - 8 : size_y], src[2 * i + 1, size_y - 8 : size_y]
            packed[1, k, i] = jnp.where(first_half, pltpu.roll(b, PAD, 0), a)
        return 0

    flat(0, own_pairs, pack)
    for dz in (-1, 1):
        held = corner_planes(dz, size_z)
        for n in range(0, len(held), 2):
            (ka, za, _), (kb, zb, _) = held[n], held[min(n + 1, len(held) - 1)]
            a, b = unit(inputs, ka), unit(inputs, kb)
            corners[0, (dz + 1) // 2, n // 2] = jnp.where(
                first_half, a[za, 0:8], pltpu.roll(b[zb, 0:8], PAD, 0)
            )
            corners[1, (dz + 1) // 2, n // 2] = jnp.where(
                first_half,
                pltpu.roll(b[zb, size_y - 8 : size_y], PAD, 0),
                a[za, size_y - 8 : size_y],
            )
    mark[0] = jnp.full((8, width), seg_z[0].astype(F32))
    mark[1] = jnp.full((8, width), seg_y[0].astype(F32))

    peers_z = 3 - (slab == 0).astype(jnp.int32) - (slab == slabs - 1).astype(jnp.int32)
    peers_y = 3 - (sub == 0).astype(jnp.int32) - (sub == subs - 1).astype(jnp.int32)
    pl.semaphore_wait(barrier, peers_z * peers_y - 1)

    copies = {}
    for side, (dz, dy) in enumerate(SIDES):
        group = []
        if dy == 0:
            for k, src in enumerate(inputs):
                low, high = REACH[k]
                if dz == 1:
                    start, to, count = size_z - low, PAD - low, low
                else:
                    start, to, count = 0, PAD + size_z, high
                if k < 2:
                    group.append(
                        (
                            src.at[:, pl.ds(start, count)],
                            halo.at[pl.ds(3 * k, 3), pl.ds(to, count)],
                        )
                    )
                else:
                    group.append((src.at[pl.ds(start, count)], halo.at[6, pl.ds(to, count)]))
        else:
            which = 0 if dy == -1 else 1
            if dz == 0:
                group.append((packed.at[which], tails.at[which]))
            else:
                tall = pl.ds(0, (len(corner_planes(dz, size_z)) + 1) // 2)
                at = (which, (dz + 1) // 2, tall)
                group.append((corners.at[at], corner_tails.at[at]))
        if (dz, dy) == (-1, 0):
            group.append((mark.at[0], marked.at[0]))
        if (dz, dy) == (0, -1):
            group.append((mark.at[1], marked.at[1]))
        group = [
            pltpu.make_async_remote_copy(
                src_ref=from_ref,
                dst_ref=to_ref,
                send_sem=send_sem.at[side, k],
                recv_sem=recv_sem.at[side, k],
                device_id=(slab + dz, sub + dy),
                device_id_type=MESH,
            )
            for k, (from_ref, to_ref) in enumerate(group)
        ]
        copies[dz, dy] = group

        @pl.when(present(dz, dy))
        def _():
            for copy in group:
                copy.start()

    def arrived(sides):
        for dz, dy in sides:

            @pl.when(present(-dz, -dy))
            def _():
                for copy in copies[dz, dy]:
                    copy.wait_recv()

    square = (parts_y * parts_x, width)
    part = lax.rem(lax.broadcasted_iota(jnp.int32, square, 0), parts_x)
    weight_x = jnp.where(seg_x[...] == part, 1.0, 0.0)
    place_x = 0.5 * (lax.broadcasted_iota(jnp.int32, square, 1) - 4 * part - 2).astype(F32)
    weight_x = jnp.concatenate([weight_x, weight_x * place_x], axis=0).astype(BF16)
    weights_x[:, 0:width] = weight_x
    weights_x[:, width : 2 * width] = weight_x
    alone = lax.dot_general(
        jnp.ones((16, width), BF16),
        weight_x,
        (((1,), (1,)), ((), ())),
        preferred_element_type=F32,
    )
    spread = square[0]
    count_x, moment_x = alone[0:1, 0:spread], alone[0:1, spread : 2 * spread]

    first_z = slab * size_z - PAD
    row = lax.broadcasted_iota(jnp.int32, (rows, width), 0)
    column = lax.broadcasted_iota(jnp.int32, (rows, width), 1)
    near = jnp.where(row < size_y + PAD, row, row - rows)
    glob_y = near + sub * size_y
    rows_in = (glob_y >= 0) & (glob_y < total_y)
    elements_in = (
        rows_in
        & (glob_y < total_y - 1)
        & (near >= -SWEEPS - 1)
        & (near < size_y + SWEEPS + 1)
        & (column < width - 1)
    )

    def left(v):
        return pltpu.roll(v, v.shape[1] - 1, 1)

    def right(v):
        return pltpu.roll(v, 1, 1)

    def lower(v):
        return pltpu.roll(v, v.shape[0] - 1, 0)

    def upper(v):
        return pltpu.roll(v, 1, 0)

    def place(k, q, main, above, below, odd):
        if odd:
            end = pltpu.roll(jnp.where(first_half, below, above), PAD, 0)
        else:
            end = jnp.where(first_half, above, below)
        value = jnp.concatenate([main, end], axis=0)
        glob_z = q + first_z
        if k < 6:
            keep = rows_in & (glob_z >= 0) & (glob_z < total_z)
            value = jnp.where(keep, value, 0.0)
            if k < 3:
                cur[k, q] = value
            else:
                right_side[k - 3, q] = value
        else:
            keep = elements_in & (glob_z >= 0) & (glob_z < total_z - 1)
            emod[q] = jnp.where(keep, value, 0.0)

    def stage_own(i, _):
        for k in range(7):
            src = unit(inputs, k)
            for odd in range(2):
                z = 2 * i + odd
                place(k, z + PAD, src[z], tails[0, k, i], tails[1, k, i], odd)
        return 0

    def stage_halo(dz):
        side = (dz + 1) // 2
        for n, (k, _, q) in enumerate(corner_planes(dz, size_z)):
            above, below = corner_tails[0, side, n // 2], corner_tails[1, side, n // 2]
            place(k, q, halo[k, q], above, below, n % 2)

    def sum_modes(q):
        e = emod[q]
        r = right(e)
        s, d = e + r, r - e
        us, ud = upper(s), upper(d)
        return s + us, us - s, d + ud, ud - d

    def invert(q, before):
        now = sum_modes(q)
        main = (LAME + 4.0 * SHEAR) / 9.0
        side = (LAME + SHEAR) / 12.0
        p = main * (now[0] + before[0])
        xy = side * (now[3] + before[3])
        xz = side * (before[2] - now[2])
        yz = side * (before[1] - now[1])
        pp = p * p
        c00 = pp - yz * yz
        c11 = pp - xz * xz
        c22 = pp - xy * xy
        c01 = xz * yz - xy * p
        c02 = xy * yz - xz * p
        c12 = xy * xz - yz * p
        det = p * c00 + xy * c01 + xz * c02
        scale = DAMPING / jnp.where(p > 0.0, det, 1.0)
        for k, entry in enumerate((c00, c11, c22, c01, c02, c12)):
            inverse[k, q] = entry * scale
        return now

    def forward(q, sweep):
        for c in range(3):
            u = cur[c, q]
            a = left(u)
            for x, t in enumerate((u + a, a - u)):
                b = lower(t)
                modes[sweep, 4 * c + 2 * x, q] = t + b
                modes[sweep, 4 * c + 2 * x + 1, q] = b - t
        return sweep

    tiles = [pl.ds(8 * tile, 8) for tile in range(rows // 8)]

    def elements(sweep, first, last, begin, add):
        for at in tiles:

            def element(q, carry):
                lo = [
                    [[modes[sweep, 4 * c + 2 * x + y, q, at] for y in range(2)] for x in range(2)]
                    for c in range(3)
                ]
                hi = [
                    [
                        [modes[sweep, 4 * c + 2 * x + y, q + 1, at] for y in range(2)]
                        for x in range(2)
                    ]
                    for c in range(3)
                ]
                out = element_modes(lo, hi, emod[q, at])
                after = []
                for c in range(3):
                    for x in range(2):
                        for y in range(2):
                            k = 4 * c + 2 * x + y
                            total, change = out[c][x][y]
                            if total is None:
                                back[sweep, k, q, at] = carry[k] - change
                                after.append(change)
                            else:
                                back[sweep, k, q, at] = carry[k] + (total - change)
                                after.append(total + change)
                return tuple(after)

            if begin:
                carry = tuple(back[sweep, k, first, at] for k in range(12))
            else:
                carry = (jnp.zeros((8, width), F32),) * 12
            carry = lax.fori_loop(first, last, element, carry, unroll=unroll)
            for k in range(12):
                if add:
                    back[sweep, k, last, at] += carry[k]
                else:
                    back[sweep, k, last, at] = carry[k]

    def image(sweep, q):
        result = []
        for c in range(3):
            halves = []
            for x in range(2):
                k = 4 * c + 2 * x
                s, d = back[sweep, k, q], back[sweep, k + 1, q]
                halves.append((s - d) + upper(s + d))
            s, d = halves
            result.append((s - d) + right(s + d))
        return result

    def finish(q, sweep):
        moved = image(sweep, q)
        r0, r1, r2 = [right_side[c, q] - moved[c] for c in range(3)]
        if sweep == SWEEPS:
            for c, value in enumerate((r0, r1, r2)):
                resid[c, q] = value
            return sweep
        i00, i11, i22, i01, i02, i12 = [inverse[k, q] for k in range(6)]
        cur[0, q] += i00 * r0 + i01 * r1 + i02 * r2
        cur[1, q] += i01 * r0 + i11 * r1 + i12 * r2
        cur[2, q] += i02 * r0 + i12 * r1 + i22 * r2
        forward(q, sweep + 1)
        return sweep

    top = PAD + size_z
    arrived([(0, -1), (0, 1)])
    flat(0, own_pairs, stage_own)
    flat(PAD, top, forward)
    flat(PAD + 1, top - 1, invert, sum_modes(PAD))
    for sweep in range(SWEEPS + 1):
        first, last = PAD + sweep, top - 1 - sweep
        elements(sweep, first, last, False, False)
        flat(first + 1, last, finish, sweep)

    result = pltpu.make_async_copy(
        cur.at[:, pl.ds(PAD, size_z), pl.ds(0, size_y)], smooth, result_sem
    )

    def group(dz, final):
        arrived([side for side in SIDES if side[0] == dz])
        stage_halo(dz)
        if dz == 1:
            flat(1, PAD, forward)
            flat(2, PAD + 1, invert, sum_modes(1))
        else:
            flat(top, planes, forward)
            flat(top - 1, planes - 1, invert, sum_modes(top - 2))
        for sweep in range(SWEEPS + 1):
            if final and sweep == SWEEPS:
                result.start()
            if dz == 1:
                elements(sweep, 1 + sweep, PAD + sweep, False, True)
                flat(2 + sweep, PAD + sweep + 1, finish, sweep)
            else:
                elements(sweep, top - 1 - sweep, planes - 1 - sweep, True, False)
                flat(top - 1 - sweep, planes - 1 - sweep, finish, sweep)

    @pl.when(lax.rem(slab, 2) == 1)
    def _():
        group(1, False)
        group(-1, True)

    @pl.when(lax.rem(slab, 2) == 0)
    def _():
        group(-1, False)
        group(1, True)

    seg_after_z = marked[0, 0:1, :]
    seg_after_y = marked[1, 0:1, :]
    maps = []
    along_z = []
    for k in range(parts_z):
        want = slab * parts_z + k
        weights = []
        places = []
        for z in range(size_z):
            weights.append(jnp.where(seg_z[z] == want, 1.0, 0.0).astype(F32))
            places.append(0.5 * (slab * size_z + z - 4 * want - 2).astype(F32))
        last = jnp.where((seg_after_z == want.astype(F32)) & (slab < slabs - 1), 1.0, 0.0)
        weights.append(last)
        places.append(0.5 * ((slab + 1) * size_z - 4 * want - 2).astype(F32))
        along_z.append((sum(weights), sum(w * p for w, p in zip(weights, places))))
        sums = [jnp.zeros((rows, width), F32) for _ in range(3)]
        turns = [jnp.zeros((rows, width), F32) for _ in range(2)]
        for z in range(size_z + 1):
            for c in range(3):
                part = weights[z] * resid[c, PAD + z]
                sums[c] = sums[c] + part
                if c < 2:
                    turns[c] = turns[c] + places[z] * part
        maps += sums + turns

    lane = lax.broadcasted_iota(jnp.int32, (2 * parts_y, rows), 1)
    part = lax.broadcasted_iota(jnp.int32, (2 * parts_y, rows), 0)
    turned = part >= parts_y
    part = jnp.where(turned, part - parts_y, part) + sub * parts_y
    segments = jnp.full((2 * parts_y, rows), -1, jnp.int32)
    for y in range(size_y):
        segments = jnp.where(lane == y, seg_y[y], segments)
    after = jnp.broadcast_to(seg_after_y[:, :rows], segments.shape)
    hit = (lane == size_y) & (after == part.astype(F32)) & (sub < subs - 1)
    weight_y = jnp.where((segments == part) | hit, 1.0, 0.0)
    place_y = 0.5 * (lane + sub * size_y - 4 * part - 2).astype(F32)
    weight_y = weight_y * jnp.where(turned, place_y, 1.0)
    along_y = jnp.sum(weight_y, axis=1, keepdims=True)

    high, low = two_parts(jnp.concatenate(maps, axis=1))
    weight_y = weight_y.astype(BF16)
    by_y = jnp.dot(weight_y, high, preferred_element_type=F32)
    by_y = by_y + jnp.dot(weight_y, low, preferred_element_type=F32)
    tall = jnp.concatenate(
        [by_y[:, width * k : width * (k + 1)] for k in range(len(maps))], axis=0
    )
    by_x = lax.dot_general(
        jnp.concatenate(two_parts(tall), axis=1),
        weights_x[...],
        (((1,), (1,)), ((), ())),
        preferred_element_type=F32,
    )
    pick = lax.broadcasted_iota(jnp.int32, (parts_y, spread), 0) == (
        lax.broadcasted_iota(jnp.int32, (parts_y, spread), 1) // parts_x
    )

    def picked(block):
        return jnp.sum(jnp.where(pick, block, 0.0), axis=0, keepdims=True)

    def chosen(k, turn_y, turn_x):
        start = (2 * k + turn_y) * parts_y
        return picked(by_x[start : start + parts_y, turn_x * spread : (turn_x + 1) * spread])

    count_y, moment_y = picked(along_y[0:parts_y]), picked(along_y[parts_y : 2 * parts_y])
    for k in range(parts_z):
        b = 5 * k
        count_z, moment_z = along_z[k]
        centre_x, centre_y, centre_z = moment_x / count_x, moment_y / count_y, moment_z / count_z
        scale = lax.rsqrt(count_x * count_y * count_z)
        s0, s1, s2 = chosen(b, 0, 0), chosen(b + 1, 0, 0), chosen(b + 2, 0, 0)
        t0 = chosen(b + 2, 1, 0) - chosen(b + 4, 0, 0) - (centre_y * s2 - centre_z * s1)
        t1 = chosen(b + 3, 0, 0) - chosen(b + 2, 0, 1) - (centre_z * s0 - centre_x * s2)
        t2 = chosen(b + 1, 0, 1) - chosen(b, 1, 0) - (centre_x * s1 - centre_y * s0)
        for c, value in enumerate((s0, s1, s2, t0, t1, t2)):
            coarse[c, k : k + 1, :] = value * scale

    for dz, dy in SIDES:

        @pl.when(present(dz, dy))
        def _():
            for copy in copies[dz, dy]:
                copy.wait_send()

    result.wait()


def on_device(field_init, load, modulus, seg_z, seg_y, seg_x):
    size_z, size_y, width = modulus.shape
    planes = size_z + 2 * PAD
    rows = size_y + 2 * PAD
    hbm = pl.BlockSpec(memory_space=pltpu.HBM)
    vmem = pl.BlockSpec(memory_space=pltpu.VMEM)
    block = (planes, rows, width)
    corner_tiles = max((len(corner_planes(dz, size_z)) + 1) // 2 for dz in (-1, 1))
    smooth, coarse = pl.pallas_call(
        functools.partial(kernel, unroll=UNROLL),
        out_shape=(
            jax.ShapeDtypeStruct((3, size_z, size_y, width), F32),
            jax.ShapeDtypeStruct((6, size_z // 4, size_y * width // 16), F32),
        ),
        in_specs=[hbm] * 6,
        out_specs=(hbm, vmem),
        scratch_shapes=[
            pltpu.SMEM(seg_z.shape, jnp.int32),
            pltpu.SMEM(seg_y.shape, jnp.int32),
            pltpu.VMEM((1, width), jnp.int32),
            pltpu.VMEM(field_init.shape, F32),
            pltpu.VMEM(load.shape, F32),
            pltpu.VMEM(modulus.shape, F32),
            pltpu.SemaphoreType.DMA((6,)),
            pltpu.SemaphoreType.DMA,
            pltpu.VMEM((2, 7, size_z // 2, 8, width), F32),
            pltpu.VMEM((2, 7, size_z // 2, 8, width), F32),
            pltpu.VMEM((2, 2, corner_tiles, 8, width), F32),
            pltpu.VMEM((2, 2, corner_tiles, 8, width), F32),
            pltpu.VMEM((7, planes, size_y, width), F32),
            pltpu.VMEM((2, 8, width), F32),
            pltpu.VMEM((2, 8, width), F32),
            pltpu.VMEM((size_y * width // 8, 2 * width), BF16),
            pltpu.VMEM((3, *block), F32),
            pltpu.VMEM((3, *block), F32),
            pltpu.VMEM(block, F32),
            pltpu.VMEM((6, *block), F32),
            pltpu.VMEM((SWEEPS + 1, 12, *block), F32),
            pltpu.VMEM((SWEEPS + 1, 12, *block), F32),
            pltpu.VMEM((3, *block), F32),
            pltpu.SemaphoreType.DMA((len(SIDES), 4)),
            pltpu.SemaphoreType.DMA((len(SIDES), 4)),
        ],
        compiler_params=pltpu.CompilerParams(
            collective_id=0, has_side_effects=True, vmem_limit_bytes=(64 << 20) - (64 << 10)
        ),
        name="sweeps",
    )(seg_z, seg_y, seg_x.reshape(1, width), field_init, load, modulus)
    return smooth, coarse


def solution(mesh):
    in_specs = (
        P(None, "slab", "sub", None),
        P(None, "slab", "sub", None),
        P("slab", "sub", None),
        P("slab"),
        P("sub"),
        P(),
    )
    out_specs = (P(None, "slab", "sub", None), P(None, "slab", "sub"))
    return jax.shard_map(
        on_device, mesh=mesh, in_specs=in_specs, out_specs=out_specs, check_vma=False
    )
```

```python
import jax
import jax.numpy as jnp
from jax import lax
from jax.experimental import pallas as pl
from jax.experimental.pallas import tpu as pltpu
from jax.sharding import PartitionSpec as P

SWEEPS = 2
DAMPING = 0.6
PAD = 4
REACH = ((SWEEPS + 1, SWEEPS + 2), (SWEEPS, SWEEPS + 1), (SWEEPS + 1, SWEEPS + 1))
POISSON = 0.3
LAME = POISSON / ((1.0 + POISSON) * (1.0 - 2.0 * POISSON))
SHEAR = 0.5 / (1.0 + POISSON)
SIDES = ((0, -1), (0, 1), (-1, 0), (1, 0), (-1, -1), (1, 1), (-1, 1), (1, -1))
MESH = pl.DeviceIdType.MESH
F32 = jnp.float32
BF16 = jnp.bfloat16


def element_modes(lo, hi, e):
    def up(c, x, y):
        return lo[c][x][y] + hi[c][x][y]

    def diff(c, x, y):
        return hi[c][x][y] - lo[c][x][y]

    e_shear = e * (SHEAR / 16.0)
    e_shear2 = e * (SHEAR / 8.0)
    e_lame = e * (LAME / 16.0)
    e_lame3 = e * (LAME / 48.0)
    e_shear3 = e * (SHEAR / 48.0)
    e_last = e * ((LAME + 4.0 * SHEAR) / 144.0)
    out = [[[[None, None], [None, None]] for _ in range(2)] for _ in range(3)]

    n0, n1, n2 = up(0, 1, 0), up(1, 0, 1), diff(2, 0, 0)
    both = e_lame * (n0 + n1 + n2)
    out[0][1][0][0] = both + e_shear2 * n0
    out[1][0][1][0] = both + e_shear2 * n1
    out[2][0][0][1] = both + e_shear2 * n2

    both = e_shear * (up(0, 0, 1) + up(1, 1, 0))
    out[0][0][1][0] = both
    out[1][1][0][0] = both
    both = e_shear * (diff(0, 0, 0) + up(2, 1, 0))
    out[0][0][0][1] = both
    out[2][1][0][0] = both
    both = e_shear * (diff(1, 0, 0) + up(2, 0, 1))
    out[1][0][0][1] = both
    out[2][0][1][0] = both

    a, b = up(0, 1, 1), diff(2, 0, 1)
    both = e_lame3 * (a + b)
    out[0][1][1][0] = both + e_shear * a
    out[2][0][1][1] = both + e_shear * b
    a, b = diff(0, 1, 0), diff(1, 0, 1)
    both = e_lame3 * (a + b)
    out[0][1][0][1] = both + e_shear * a
    out[1][0][1][1] = both + e_shear * b
    a, b = up(1, 1, 1), diff(2, 1, 0)
    both = e_lame3 * (a + b)
    out[1][1][1][0] = both + e_shear * a
    out[2][1][0][1] = both + e_shear * b

    a, b, c = diff(0, 0, 1), diff(1, 1, 0), up(2, 1, 1)
    both = a + b + c
    out[0][0][1][1] = e_shear3 * (both + a)
    out[1][1][0][1] = e_shear3 * (both + b)
    out[2][1][1][0] = e_shear3 * (both + c)

    for c in range(3):
        out[c][1][1][1] = e_last * diff(c, 1, 1)
    return out


def corner_planes(dz, size_z):
    held = []
    for k in range(7):
        low, high = REACH[k // 3]
        if dz == 1:
            held += [(k, size_z - low + i, PAD - low + i) for i in range(low)]
        else:
            held += [(k, i, PAD + size_z + i) for i in range(high)]
    return held


def two_parts(v):
    high = v.astype(BF16)
    return high, (v - high.astype(F32)).astype(BF16)


def flat(first, last, body, carry=0):
    for q in range(first, last):
        carry = body(q, carry)
    return carry


def kernel(
    seg_z_hbm,
    seg_y_hbm,
    seg_x_hbm,
    field_hbm,
    load_hbm,
    mod_hbm,
    smooth,
    coarse,
    seg_z,
    seg_y,
    seg_x,
    field,
    load,
    mod,
    correction,
    own_sem,
    result_sem,
    packed,
    tails,
    corners,
    corner_tails,
    halo,
    mark,
    marked,
    weights_x,
    cur,
    right_side,
    emod,
    inverse,
    modes,
    back,
    resid,
    send_sem,
    recv_sem,
):
    size_z, size_y, width = smooth.shape[1:]
    planes, rows = cur.shape[1], cur.shape[2]
    slab, sub = lax.axis_index("slab"), lax.axis_index("sub")
    slabs, subs = lax.axis_size("slab"), lax.axis_size("sub")
    total_z, total_y = size_z * slabs, size_y * subs
    parts_z, parts_y, parts_x = size_z // 4, size_y // 4, width // 4
    own_pairs = size_z // 2

    def present(dz, dy):
        there = jnp.bool_(True)
        if dz == 1:
            there = there & (slab < slabs - 1)
        if dz == -1:
            there = there & (slab > 0)
        if dy == 1:
            there = there & (sub < subs - 1)
        if dy == -1:
            there = there & (sub > 0)
        return there

    barrier = pltpu.get_barrier_semaphore()
    for dz, dy in SIDES:

        @pl.when(present(dz, dy))
        def _():
            pl.semaphore_signal(
                barrier, inc=1, device_id=(slab + dz, sub + dy), device_id_type=MESH
            )

    own = [
        pltpu.make_async_copy(src, dst, own_sem.at[k])
        for k, (src, dst) in enumerate(
            (
                (field_hbm, field),
                (load_hbm, load),
                (mod_hbm, mod),
                (seg_z_hbm, seg_z),
                (seg_y_hbm, seg_y),
                (seg_x_hbm, seg_x),
            )
        )
    ]
    for copy in own:
        copy.start()
    for copy in own:
        copy.wait()

    first_half = lax.broadcasted_iota(jnp.int32, (8, width), 0) < PAD

    def unit(refs, k):
        return refs[k // 3].at[k % 3] if k < 6 else refs[2]

    inputs = (field, load, mod)

    def pack(i, _):
        for k in range(7):
            src = unit(inputs, k)
            a, b = src[2 * i, 0:8], src[2 * i + 1, 0:8]
            packed[0, k, i] = jnp.where(first_half, a, pltpu.roll(b, PAD, 0))
            a, b = src[2 * i, size_y - 8 : size_y], src[2 * i + 1, size_y - 8 : size_y]
            packed[1, k, i] = jnp.where(first_half, pltpu.roll(b, PAD, 0), a)
        return 0

    flat(0, own_pairs, pack)
    for dz in (-1, 1):
        held = corner_planes(dz, size_z)
        for n in range(0, len(held), 2):
            (ka, za, _), (kb, zb, _) = held[n], held[min(n + 1, len(held) - 1)]
            a, b = unit(inputs, ka), unit(inputs, kb)
            corners[0, (dz + 1) // 2, n // 2] = jnp.where(
                first_half, a[za, 0:8], pltpu.roll(b[zb, 0:8], PAD, 0)
            )
            corners[1, (dz + 1) // 2, n // 2] = jnp.where(
                first_half,
                pltpu.roll(b[zb, size_y - 8 : size_y], PAD, 0),
                a[za, size_y - 8 : size_y],
            )
    mark[0] = jnp.full((8, width), seg_z[0].astype(F32))
    mark[1] = jnp.full((8, width), seg_y[0].astype(F32))

    peers_z = 3 - (slab == 0).astype(jnp.int32) - (slab == slabs - 1).astype(jnp.int32)
    peers_y = 3 - (sub == 0).astype(jnp.int32) - (sub == subs - 1).astype(jnp.int32)
    pl.semaphore_wait(barrier, peers_z * peers_y - 1)

    copies = {}
    for side, (dz, dy) in enumerate(SIDES):
        group = []
        if dy == 0:
            for k, src in enumerate(inputs):
                low, high = REACH[k]
                if dz == 1:
                    start, to, count = size_z - low, PAD - low, low
                else:
                    start, to, count = 0, PAD + size_z, high
                if k < 2:
                    group.append(
                        (
                            src.at[:, pl.ds(start, count)],
                            halo.at[pl.ds(3 * k, 3), pl.ds(to, count)],
                        )
                    )
                else:
                    group.append((src.at[pl.ds(start, count)], halo.at[6, pl.ds(to, count)]))
        else:
            which = 0 if dy == -1 else 1
            if dz == 0:
                group.append((packed.at[which], tails.at[which]))
            else:
                tall = pl.ds(0, (len(corner_planes(dz, size_z)) + 1) // 2)
                at = (which, (dz + 1) // 2, tall)
                group.append((corners.at[at], corner_tails.at[at]))
        if (dz, dy) == (-1, 0):
            group.append((mark.at[0], marked.at[0]))
        if (dz, dy) == (0, -1):
            group.append((mark.at[1], marked.at[1]))
        group = [
            pltpu.make_async_remote_copy(
                src_ref=from_ref,
                dst_ref=to_ref,
                send_sem=send_sem.at[side, k],
                recv_sem=recv_sem.at[side, k],
                device_id=(slab + dz, sub + dy),
                device_id_type=MESH,
            )
            for k, (from_ref, to_ref) in enumerate(group)
        ]
        copies[dz, dy] = group

        @pl.when(present(dz, dy))
        def _():
            for copy in group:
                copy.start()

    def arrived(sides):
        for dz, dy in sides:

            @pl.when(present(-dz, -dy))
            def _():
                for copy in copies[dz, dy]:
                    copy.wait_recv()

    square = (parts_y * parts_x, width)
    part = lax.rem(lax.broadcasted_iota(jnp.int32, square, 0), parts_x)
    weight_x = jnp.where(seg_x[...] == part, 1.0, 0.0)
    place_x = 0.5 * (lax.broadcasted_iota(jnp.int32, square, 1) - 4 * part - 2).astype(F32)
    weight_x = jnp.concatenate([weight_x, weight_x * place_x], axis=0).astype(BF16)
    weights_x[:, 0:width] = weight_x
    weights_x[:, width : 2 * width] = weight_x
    alone = lax.dot_general(
        jnp.ones((16, width), BF16),
        weight_x,
        (((1,), (1,)), ((), ())),
        preferred_element_type=F32,
    )
    spread = square[0]
    count_x, moment_x = alone[0:1, 0:spread], alone[0:1, spread : 2 * spread]

    first_z = slab * size_z - PAD
    row = lax.broadcasted_iota(jnp.int32, (rows, width), 0)
    column = lax.broadcasted_iota(jnp.int32, (rows, width), 1)
    near = jnp.where(row < size_y + PAD, row, row - rows)
    glob_y = near + sub * size_y
    rows_in = (glob_y >= 0) & (glob_y < total_y)
    elements_in = (
        rows_in
        & (glob_y < total_y - 1)
        & (near >= -SWEEPS - 1)
        & (near < size_y + SWEEPS + 1)
        & (column < width - 1)
    )

    def left(v):
        return pltpu.roll(v, v.shape[1] - 1, 1)

    def right(v):
        return pltpu.roll(v, 1, 1)

    def lower(v):
        return pltpu.roll(v, v.shape[0] - 1, 0)

    def upper(v):
        return pltpu.roll(v, 1, 0)

    def place(k, q, main, above, below, odd):
        if odd:
            end = pltpu.roll(jnp.where(first_half, below, above), PAD, 0)
        else:
            end = jnp.where(first_half, above, below)
        value = jnp.concatenate([main, end], axis=0)
        glob_z = q + first_z
        if k < 6:
            keep = rows_in & (glob_z >= 0) & (glob_z < total_z)
            value = jnp.where(keep, value, 0.0)
            if k < 3:
                cur[k, q] = value
            else:
                right_side[k - 3, q] = value
        else:
            keep = elements_in & (glob_z >= 0) & (glob_z < total_z - 1)
            emod[q] = jnp.where(keep, value, 0.0)

    def stage_own(i, _):
        for k in range(7):
            src = unit(inputs, k)
            for odd in range(2):
                z = 2 * i + odd
                place(k, z + PAD, src[z], tails[0, k, i], tails[1, k, i], odd)
        return 0

    def stage_halo(dz):
        side = (dz + 1) // 2
        for n, (k, _, q) in enumerate(corner_planes(dz, size_z)):
            above, below = corner_tails[0, side, n // 2], corner_tails[1, side, n // 2]
            place(k, q, halo[k, q], above, below, n % 2)

    def sum_modes(q):
        e = emod[q]
        r = right(e)
        s, d = e + r, r - e
        us, ud = upper(s), upper(d)
        return s + us, us - s, d + ud, ud - d

    def invert(q, before):
        now = sum_modes(q)
        main = (LAME + 4.0 * SHEAR) / 9.0
        side = (LAME + SHEAR) / 12.0
        p = main * (now[0] + before[0])
        xy = side * (now[3] + before[3])
        xz = side * (before[2] - now[2])
        yz = side * (before[1] - now[1])
        pp = p * p
        c00 = pp - yz * yz
        c11 = pp - xz * xz
        c22 = pp - xy * xy
        c01 = xz * yz - xy * p
        c02 = xy * yz - xz * p
        c12 = xy * xz - yz * p
        det = p * c00 + xy * c01 + xz * c02
        scale = DAMPING / jnp.where(p > 0.0, det, 1.0)
        for k, entry in enumerate((c00, c11, c22, c01, c02, c12)):
            inverse[k, q] = entry * scale
        return now

    def forward(q, sweep):
        for c in range(3):
            u = cur[c, q]
            a = left(u)
            for x, t in enumerate((u + a, a - u)):
                b = lower(t)
                modes[sweep, 4 * c + 2 * x, q] = t + b
                modes[sweep, 4 * c + 2 * x + 1, q] = b - t
        return sweep

    tiles = [pl.ds(8 * tile, 8) for tile in range(rows // 8)]

    def elements(sweep, first, last, begin, add):
        for at in tiles:

            def element(q, carry):
                lo = [
                    [[modes[sweep, 4 * c + 2 * x + y, q, at] for y in range(2)] for x in range(2)]
                    for c in range(3)
                ]
                hi = [
                    [
                        [modes[sweep, 4 * c + 2 * x + y, q + 1, at] for y in range(2)]
                        for x in range(2)
                    ]
                    for c in range(3)
                ]
                out = element_modes(lo, hi, emod[q, at])
                after = []
                for c in range(3):
                    for x in range(2):
                        for y in range(2):
                            k = 4 * c + 2 * x + y
                            total, change = out[c][x][y]
                            if total is None:
                                back[sweep, k, q, at] = carry[k] - change
                                after.append(change)
                            else:
                                back[sweep, k, q, at] = carry[k] + (total - change)
                                after.append(total + change)
                return tuple(after)

            if begin:
                carry = tuple(back[sweep, k, first, at] for k in range(12))
            else:
                carry = (jnp.zeros((8, width), F32),) * 12
            carry = flat(first, last, element, carry)
            for k in range(12):
                if add:
                    back[sweep, k, last, at] += carry[k]
                else:
                    back[sweep, k, last, at] = carry[k]

    def image(sweep, q):
        result = []
        for c in range(3):
            halves = []
            for x in range(2):
                k = 4 * c + 2 * x
                s, d = back[sweep, k, q], back[sweep, k + 1, q]
                halves.append((s - d) + upper(s + d))
            s, d = halves
            result.append((s - d) + right(s + d))
        return result

    def finish(q, sweep):
        moved = image(sweep, q)
        r0, r1, r2 = [right_side[c, q] - moved[c] for c in range(3)]
        if sweep == SWEEPS:
            for c, value in enumerate((r0, r1, r2)):
                resid[c, q] = value
            return sweep
        i00, i11, i22, i01, i02, i12 = [inverse[k, q] for k in range(6)]
        cur[0, q] += i00 * r0 + i01 * r1 + i02 * r2
        cur[1, q] += i01 * r0 + i11 * r1 + i12 * r2
        cur[2, q] += i02 * r0 + i12 * r1 + i22 * r2
        forward(q, sweep + 1)
        return sweep

    top = PAD + size_z
    arrived([(0, -1), (0, 1)])
    flat(0, own_pairs, stage_own)
    flat(PAD, top, forward)
    flat(PAD + 1, top - 1, invert, sum_modes(PAD))
    for sweep in range(SWEEPS + 1):
        first, last = PAD + sweep, top - 1 - sweep
        elements(sweep, first, last, False, False)
        flat(first + 1, last, finish, sweep)

    arrived([side for side in SIDES if side[0] != 0])
    stage_halo(1)
    stage_halo(-1)
    flat(1, PAD, forward)
    flat(top, planes, forward)
    flat(2, PAD + 1, invert, sum_modes(1))
    flat(top - 1, planes - 1, invert, sum_modes(top - 2))
    result = pltpu.make_async_copy(
        correction, smooth, result_sem
    )
    for sweep in range(SWEEPS + 1):
        if sweep == SWEEPS:
            for c in range(3):
                for z in range(size_z):
                    correction[c, z] = cur[c, PAD + z, 0:size_y] - field[c, z]
            result.start()
        elements(sweep, 1 + sweep, PAD + sweep, False, True)
        elements(sweep, top - 1 - sweep, planes - 1 - sweep, True, False)
        flat(2 + sweep, PAD + sweep + 1, finish, sweep)
        flat(top - 1 - sweep, planes - 1 - sweep, finish, sweep)
    seg_after_z = marked[0, 0:1, :]
    seg_after_y = marked[1, 0:1, :]
    maps = []
    along_z = []
    for k in range(parts_z):
        want = slab * parts_z + k
        weights = []
        places = []
        for z in range(size_z):
            weights.append(jnp.where(seg_z[z] == want, 1.0, 0.0).astype(F32))
            places.append(0.5 * (slab * size_z + z - 4 * want - 2).astype(F32))
        last = jnp.where((seg_after_z == want.astype(F32)) & (slab < slabs - 1), 1.0, 0.0)
        weights.append(last)
        places.append(0.5 * ((slab + 1) * size_z - 4 * want - 2).astype(F32))
        along_z.append((sum(weights), sum(w * p for w, p in zip(weights, places))))
        sums = [jnp.zeros((rows, width), F32) for _ in range(3)]
        turns = [jnp.zeros((rows, width), F32) for _ in range(2)]
        for z in range(size_z + 1):
            for c in range(3):
                part = weights[z] * resid[c, PAD + z]
                sums[c] = sums[c] + part
                if c < 2:
                    turns[c] = turns[c] + places[z] * part
        maps += sums + turns

    lane = lax.broadcasted_iota(jnp.int32, (2 * parts_y, rows), 1)
    part = lax.broadcasted_iota(jnp.int32, (2 * parts_y, rows), 0)
    turned = part >= parts_y
    part = jnp.where(turned, part - parts_y, part) + sub * parts_y
    segments = jnp.full((2 * parts_y, rows), -1, jnp.int32)
    for y in range(size_y):
        segments = jnp.where(lane == y, seg_y[y], segments)
    after = jnp.broadcast_to(seg_after_y[:, :rows], segments.shape)
    hit = (lane == size_y) & (after == part.astype(F32)) & (sub < subs - 1)
    weight_y = jnp.where((segments == part) | hit, 1.0, 0.0)
    place_y = 0.5 * (lane + sub * size_y - 4 * part - 2).astype(F32)
    weight_y = weight_y * jnp.where(turned, place_y, 1.0)
    along_y = jnp.sum(weight_y, axis=1, keepdims=True)

    high, low = two_parts(jnp.concatenate(maps, axis=1))
    weight_y = weight_y.astype(BF16)
    by_y = jnp.dot(weight_y, high, preferred_element_type=F32)
    by_y = by_y + jnp.dot(weight_y, low, preferred_element_type=F32)
    tall = jnp.concatenate(
        [by_y[:, width * k : width * (k + 1)] for k in range(len(maps))], axis=0
    )
    by_x = lax.dot_general(
        jnp.concatenate(two_parts(tall), axis=1),
        weights_x[...],
        (((1,), (1,)), ((), ())),
        preferred_element_type=F32,
    )
    pick = lax.broadcasted_iota(jnp.int32, (parts_y, spread), 0) == (
        lax.broadcasted_iota(jnp.int32, (parts_y, spread), 1) // parts_x
    )

    def picked(block):
        return jnp.sum(jnp.where(pick, block, 0.0), axis=0, keepdims=True)

    def chosen(k, turn_y, turn_x):
        start = (2 * k + turn_y) * parts_y
        return picked(by_x[start : start + parts_y, turn_x * spread : (turn_x + 1) * spread])

    count_y, moment_y = picked(along_y[0:parts_y]), picked(along_y[parts_y : 2 * parts_y])
    for k in range(parts_z):
        b = 5 * k
        count_z, moment_z = along_z[k]
        centre_x, centre_y, centre_z = moment_x / count_x, moment_y / count_y, moment_z / count_z
        scale = lax.rsqrt(count_x * count_y * count_z)
        s0, s1, s2 = chosen(b, 0, 0), chosen(b + 1, 0, 0), chosen(b + 2, 0, 0)
        t0 = chosen(b + 2, 1, 0) - chosen(b + 4, 0, 0) - (centre_y * s2 - centre_z * s1)
        t1 = chosen(b + 3, 0, 0) - chosen(b + 2, 0, 1) - (centre_z * s0 - centre_x * s2)
        t2 = chosen(b + 1, 0, 1) - chosen(b, 1, 0) - (centre_x * s1 - centre_y * s0)
        for c, value in enumerate((s0, s1, s2, t0, t1, t2)):
            coarse[c, k : k + 1, :] = value * scale

    for dz, dy in SIDES:

        @pl.when(present(dz, dy))
        def _():
            for copy in copies[dz, dy]:
                copy.wait_send()

    result.wait()


def on_device(field_init, load, modulus, seg_z, seg_y, seg_x):
    size_z, size_y, width = modulus.shape
    planes = size_z + 2 * PAD
    rows = size_y + 2 * PAD
    hbm = pl.BlockSpec(memory_space=pltpu.HBM)
    vmem = pl.BlockSpec(memory_space=pltpu.VMEM)
    block = (planes, rows, width)
    corner_tiles = max((len(corner_planes(dz, size_z)) + 1) // 2 for dz in (-1, 1))
    smooth, coarse = pl.pallas_call(
        kernel,
        out_shape=(
            jax.ShapeDtypeStruct((3, size_z, size_y, width), F32),
            jax.ShapeDtypeStruct((6, size_z // 4, size_y * width // 16), F32),
        ),
        in_specs=[hbm] * 6,
        out_specs=(hbm, vmem),
        scratch_shapes=[
            pltpu.SMEM(seg_z.shape, jnp.int32),
            pltpu.SMEM(seg_y.shape, jnp.int32),
            pltpu.VMEM((1, width), jnp.int32),
            pltpu.VMEM(field_init.shape, F32),
            pltpu.VMEM(load.shape, F32),
            pltpu.VMEM(modulus.shape, F32),
            pltpu.VMEM(field_init.shape, F32),
            pltpu.SemaphoreType.DMA((6,)),
            pltpu.SemaphoreType.DMA,
            pltpu.VMEM((2, 7, size_z // 2, 8, width), F32),
            pltpu.VMEM((2, 7, size_z // 2, 8, width), F32),
            pltpu.VMEM((2, 2, corner_tiles, 8, width), F32),
            pltpu.VMEM((2, 2, corner_tiles, 8, width), F32),
            pltpu.VMEM((7, planes, size_y, width), F32),
            pltpu.VMEM((2, 8, width), F32),
            pltpu.VMEM((2, 8, width), F32),
            pltpu.VMEM((size_y * width // 8, 2 * width), BF16),
            pltpu.VMEM((3, *block), F32),
            pltpu.VMEM((3, *block), F32),
            pltpu.VMEM(block, F32),
            pltpu.VMEM((6, *block), F32),
            pltpu.VMEM((SWEEPS + 1, 12, *block), F32),
            pltpu.VMEM((SWEEPS + 1, 12, *block), F32),
            pltpu.VMEM((3, *block), F32),
            pltpu.SemaphoreType.DMA((len(SIDES), 4)),
            pltpu.SemaphoreType.DMA((len(SIDES), 4)),
        ],
        compiler_params=pltpu.CompilerParams(
            collective_id=0, has_side_effects=True, vmem_limit_bytes=(64 << 20) - (64 << 10)
        ),
        name="sweeps",
    )(seg_z, seg_y, seg_x.reshape(1, width), field_init, load, modulus)
    return field_init + smooth, coarse


def solution(mesh):
    in_specs = (
        P(None, "slab", "sub", None),
        P(None, "slab", "sub", None),
        P("slab", "sub", None),
        P("slab"),
        P("sub"),
        P(),
    )
    out_specs = (P(None, "slab", "sub", None), P(None, "slab", "sub"))
    return jax.shard_map(
        on_device, mesh=mesh, in_specs=in_specs, out_specs=out_specs, check_vma=False
    )
```

```python
import functools

import jax
import jax.numpy as jnp
from jax import lax
from jax.experimental import pallas as pl
from jax.experimental.pallas import tpu as pltpu
from jax.sharding import PartitionSpec as P

SWEEPS = 2
DAMPING = 0.6
PAD = 4
REACH = ((SWEEPS + 1, SWEEPS + 2), (SWEEPS, SWEEPS + 1), (SWEEPS + 1, SWEEPS + 1))
POISSON = 0.3
LAME = POISSON / ((1.0 + POISSON) * (1.0 - 2.0 * POISSON))
SHEAR = 0.5 / (1.0 + POISSON)
SIDES = ((0, -1), (0, 1), (-1, 0), (1, 0), (-1, -1), (1, 1), (-1, 1), (1, -1))
UNROLL = 1
MESH = pl.DeviceIdType.MESH
F32 = jnp.float32
BF16 = jnp.bfloat16


def element_modes(lo, hi, e):
    def up(c, x, y):
        return lo[c][x][y] + hi[c][x][y]

    def diff(c, x, y):
        return hi[c][x][y] - lo[c][x][y]

    e_shear = e * (SHEAR / 16.0)
    e_shear2 = e * (SHEAR / 8.0)
    e_lame = e * (LAME / 16.0)
    e_lame3 = e * (LAME / 48.0)
    e_shear3 = e * (SHEAR / 48.0)
    e_last = e * ((LAME + 4.0 * SHEAR) / 144.0)
    out = [[[[None, None], [None, None]] for _ in range(2)] for _ in range(3)]

    n0, n1, n2 = up(0, 1, 0), up(1, 0, 1), diff(2, 0, 0)
    both = e_lame * (n0 + n1 + n2)
    out[0][1][0][0] = both + e_shear2 * n0
    out[1][0][1][0] = both + e_shear2 * n1
    out[2][0][0][1] = both + e_shear2 * n2

    both = e_shear * (up(0, 0, 1) + up(1, 1, 0))
    out[0][0][1][0] = both
    out[1][1][0][0] = both
    both = e_shear * (diff(0, 0, 0) + up(2, 1, 0))
    out[0][0][0][1] = both
    out[2][1][0][0] = both
    both = e_shear * (diff(1, 0, 0) + up(2, 0, 1))
    out[1][0][0][1] = both
    out[2][0][1][0] = both

    a, b = up(0, 1, 1), diff(2, 0, 1)
    both = e_lame3 * (a + b)
    out[0][1][1][0] = both + e_shear * a
    out[2][0][1][1] = both + e_shear * b
    a, b = diff(0, 1, 0), diff(1, 0, 1)
    both = e_lame3 * (a + b)
    out[0][1][0][1] = both + e_shear * a
    out[1][0][1][1] = both + e_shear * b
    a, b = up(1, 1, 1), diff(2, 1, 0)
    both = e_lame3 * (a + b)
    out[1][1][1][0] = both + e_shear * a
    out[2][1][0][1] = both + e_shear * b

    a, b, c = diff(0, 0, 1), diff(1, 1, 0), up(2, 1, 1)
    both = a + b + c
    out[0][0][1][1] = e_shear3 * (both + a)
    out[1][1][0][1] = e_shear3 * (both + b)
    out[2][1][1][0] = e_shear3 * (both + c)

    for c in range(3):
        out[c][1][1][1] = e_last * diff(c, 1, 1)
    return out


def corner_planes(dz, size_z):
    held = []
    for k in range(7):
        low, high = REACH[k // 3]
        if dz == 1:
            held += [(k, size_z - low + i, PAD - low + i) for i in range(low)]
        else:
            held += [(k, i, PAD + size_z + i) for i in range(high)]
    return held


def two_parts(v):
    high = v.astype(BF16)
    return high, (v - high.astype(F32)).astype(BF16)


def flat(first, last, body, carry=0):
    for q in range(first, last):
        carry = body(q, carry)
    return carry


def kernel(
    seg_z_hbm,
    seg_y_hbm,
    seg_x_hbm,
    field_hbm,
    load_hbm,
    mod_hbm,
    smooth,
    coarse,
    seg_z,
    seg_y,
    seg_x,
    field,
    load,
    mod,
    own_sem,
    result_sem,
    packed,
    tails,
    corners,
    corner_tails,
    halo,
    mark,
    marked,
    weights_x,
    cur,
    right_side,
    emod,
    inverse,
    modes,
    back,
    resid,
    send_sem,
    recv_sem,
    *,
    unroll,
):
    size_z, size_y, width = smooth.shape[1:]
    planes, rows = cur.shape[1], cur.shape[2]
    slab, sub = lax.axis_index("slab"), lax.axis_index("sub")
    slabs, subs = lax.axis_size("slab"), lax.axis_size("sub")
    total_z, total_y = size_z * slabs, size_y * subs
    parts_z, parts_y, parts_x = size_z // 4, size_y // 4, width // 4
    own_pairs = size_z // 2

    def present(dz, dy):
        there = jnp.bool_(True)
        if dz == 1:
            there = there & (slab < slabs - 1)
        if dz == -1:
            there = there & (slab > 0)
        if dy == 1:
            there = there & (sub < subs - 1)
        if dy == -1:
            there = there & (sub > 0)
        return there

    barrier = pltpu.get_barrier_semaphore()
    for dz, dy in SIDES:

        @pl.when(present(dz, dy))
        def _():
            pl.semaphore_signal(
                barrier, inc=1, device_id=(slab + dz, sub + dy), device_id_type=MESH
            )

    own = [
        pltpu.make_async_copy(src, dst, own_sem.at[k])
        for k, (src, dst) in enumerate(
            (
                (field_hbm, field),
                (load_hbm, load),
                (mod_hbm, mod),
                (seg_z_hbm, seg_z),
                (seg_y_hbm, seg_y),
                (seg_x_hbm, seg_x),
            )
        )
    ]
    for copy in own:
        copy.start()
    for copy in own:
        copy.wait()

    first_half = lax.broadcasted_iota(jnp.int32, (8, width), 0) < PAD

    def unit(refs, k):
        return refs[k // 3].at[k % 3] if k < 6 else refs[2]

    inputs = (field, load, mod)

    def pack(i, _):
        for k in range(7):
            src = unit(inputs, k)
            a, b = src[2 * i, 0:8], src[2 * i + 1, 0:8]
            packed[0, k, i] = jnp.where(first_half, a, pltpu.roll(b, PAD, 0))
            a, b = src[2 * i, size_y - 8 : size_y], src[2 * i + 1, size_y - 8 : size_y]
            packed[1, k, i] = jnp.where(first_half, pltpu.roll(b, PAD, 0), a)
        return 0

    flat(0, own_pairs, pack)
    for dz in (-1, 1):
        held = corner_planes(dz, size_z)
        for n in range(0, len(held), 2):
            (ka, za, _), (kb, zb, _) = held[n], held[min(n + 1, len(held) - 1)]
            a, b = unit(inputs, ka), unit(inputs, kb)
            corners[0, (dz + 1) // 2, n // 2] = jnp.where(
                first_half, a[za, 0:8], pltpu.roll(b[zb, 0:8], PAD, 0)
            )
            corners[1, (dz + 1) // 2, n // 2] = jnp.where(
                first_half,
                pltpu.roll(b[zb, size_y - 8 : size_y], PAD, 0),
                a[za, size_y - 8 : size_y],
            )
    mark[0] = jnp.full((8, width), seg_z[0].astype(F32))
    mark[1] = jnp.full((8, width), seg_y[0].astype(F32))

    peers_z = 3 - (slab == 0).astype(jnp.int32) - (slab == slabs - 1).astype(jnp.int32)
    peers_y = 3 - (sub == 0).astype(jnp.int32) - (sub == subs - 1).astype(jnp.int32)
    pl.semaphore_wait(barrier, peers_z * peers_y - 1)

    copies = {}
    for side, (dz, dy) in enumerate(SIDES):
        group = []
        if dy == 0:
            for k, src in enumerate(inputs):
                low, high = REACH[k]
                if dz == 1:
                    start, to, count = size_z - low, PAD - low, low
                else:
                    start, to, count = 0, PAD + size_z, high
                if k < 2:
                    group.append(
                        (
                            src.at[:, pl.ds(start, count)],
                            halo.at[pl.ds(3 * k, 3), pl.ds(to, count)],
                        )
                    )
                else:
                    group.append((src.at[pl.ds(start, count)], halo.at[6, pl.ds(to, count)]))
        else:
            which = 0 if dy == -1 else 1
            if dz == 0:
                group.append((packed.at[which], tails.at[which]))
            else:
                tall = pl.ds(0, (len(corner_planes(dz, size_z)) + 1) // 2)
                at = (which, (dz + 1) // 2, tall)
                group.append((corners.at[at], corner_tails.at[at]))
        if (dz, dy) == (-1, 0):
            group.append((mark.at[0], marked.at[0]))
        if (dz, dy) == (0, -1):
            group.append((mark.at[1], marked.at[1]))
        group = [
            pltpu.make_async_remote_copy(
                src_ref=from_ref,
                dst_ref=to_ref,
                send_sem=send_sem.at[side, k],
                recv_sem=recv_sem.at[side, k],
                device_id=(slab + dz, sub + dy),
                device_id_type=MESH,
            )
            for k, (from_ref, to_ref) in enumerate(group)
        ]
        copies[dz, dy] = group

        @pl.when(present(dz, dy))
        def _():
            for copy in group:
                copy.start()

    def arrived(sides):
        for dz, dy in sides:

            @pl.when(present(-dz, -dy))
            def _():
                for copy in copies[dz, dy]:
                    copy.wait_recv()

    square = (parts_y * parts_x, width)
    part = lax.rem(lax.broadcasted_iota(jnp.int32, square, 0), parts_x)
    weight_x = jnp.where(seg_x[...] == part, 1.0, 0.0)
    place_x = 0.5 * (lax.broadcasted_iota(jnp.int32, square, 1) - 4 * part - 2).astype(F32)
    weight_x = jnp.concatenate([weight_x, weight_x * place_x], axis=0).astype(BF16)
    weights_x[:, 0:width] = weight_x
    weights_x[:, width : 2 * width] = weight_x
    alone = lax.dot_general(
        jnp.ones((16, width), BF16),
        weight_x,
        (((1,), (1,)), ((), ())),
        preferred_element_type=F32,
    )
    spread = square[0]
    count_x, moment_x = alone[0:1, 0:spread], alone[0:1, spread : 2 * spread]

    first_z = slab * size_z - PAD
    row = lax.broadcasted_iota(jnp.int32, (rows, width), 0)
    column = lax.broadcasted_iota(jnp.int32, (rows, width), 1)
    near = jnp.where(row < size_y + PAD, row, row - rows)
    glob_y = near + sub * size_y
    rows_in = (glob_y >= 0) & (glob_y < total_y)
    elements_in = (
        rows_in
        & (glob_y < total_y - 1)
        & (near >= -SWEEPS - 1)
        & (near < size_y + SWEEPS + 1)
        & (column < width - 1)
    )

    def left(v):
        return pltpu.roll(v, v.shape[1] - 1, 1)

    def right(v):
        return pltpu.roll(v, 1, 1)

    def lower(v):
        return pltpu.roll(v, v.shape[0] - 1, 0)

    def upper(v):
        return pltpu.roll(v, 1, 0)

    def place(k, q, main, above, below, odd):
        if odd:
            end = pltpu.roll(jnp.where(first_half, below, above), PAD, 0)
        else:
            end = jnp.where(first_half, above, below)
        value = jnp.concatenate([main, end], axis=0)
        glob_z = q + first_z
        if k < 6:
            keep = rows_in & (glob_z >= 0) & (glob_z < total_z)
            value = jnp.where(keep, value, 0.0)
            if k < 3:
                cur[k, q] = value
            else:
                right_side[k - 3, q] = value
        else:
            keep = elements_in & (glob_z >= 0) & (glob_z < total_z - 1)
            emod[q] = jnp.where(keep, value, 0.0)

    def stage_own(i, _):
        for k in range(7):
            src = unit(inputs, k)
            for odd in range(2):
                z = 2 * i + odd
                place(k, z + PAD, src[z], tails[0, k, i], tails[1, k, i], odd)
        return 0

    def stage_halo(dz):
        side = (dz + 1) // 2
        for n, (k, _, q) in enumerate(corner_planes(dz, size_z)):
            above, below = corner_tails[0, side, n // 2], corner_tails[1, side, n // 2]
            place(k, q, halo[k, q], above, below, n % 2)

    def sum_modes(q):
        e = emod[q]
        r = right(e)
        s, d = e + r, r - e
        us, ud = upper(s), upper(d)
        return s + us, us - s, d + ud, ud - d

    def invert(q, before):
        now = sum_modes(q)
        main = (LAME + 4.0 * SHEAR) / 9.0
        side = (LAME + SHEAR) / 12.0
        p = main * (now[0] + before[0])
        xy = side * (now[3] + before[3])
        xz = side * (before[2] - now[2])
        yz = side * (before[1] - now[1])
        pp = p * p
        c00 = pp - yz * yz
        c11 = pp - xz * xz
        c22 = pp - xy * xy
        c01 = xz * yz - xy * p
        c02 = xy * yz - xz * p
        c12 = xy * xz - yz * p
        det = p * c00 + xy * c01 + xz * c02
        scale = DAMPING / jnp.where(p > 0.0, det, 1.0)
        for k, entry in enumerate((c00, c11, c22, c01, c02, c12)):
            inverse[k, q] = entry * scale
        return now

    def forward(q, sweep):
        for c in range(3):
            u = cur[c, q]
            a = left(u)
            for x, t in enumerate((u + a, a - u)):
                b = lower(t)
                modes[sweep, 4 * c + 2 * x, q] = t + b
                modes[sweep, 4 * c + 2 * x + 1, q] = b - t
        return sweep

    tiles = [pl.ds(8 * tile, 8) for tile in range(rows // 8)]

    def elements(sweep, first, last, begin, add):
        for at in tiles:

            def element(q, carry):
                lo = [
                    [[modes[sweep, 4 * c + 2 * x + y, q, at] for y in range(2)] for x in range(2)]
                    for c in range(3)
                ]
                hi = [
                    [
                        [modes[sweep, 4 * c + 2 * x + y, q + 1, at] for y in range(2)]
                        for x in range(2)
                    ]
                    for c in range(3)
                ]
                out = element_modes(lo, hi, emod[q, at])
                after = []
                for c in range(3):
                    for x in range(2):
                        for y in range(2):
                            k = 4 * c + 2 * x + y
                            total, change = out[c][x][y]
                            if total is None:
                                back[sweep, k, q, at] = carry[k] - change
                                after.append(change)
                            else:
                                back[sweep, k, q, at] = carry[k] + (total - change)
                                after.append(total + change)
                return tuple(after)

            if begin:
                carry = tuple(back[sweep, k, first, at] for k in range(12))
            else:
                carry = (jnp.zeros((8, width), F32),) * 12
            carry = lax.fori_loop(first, last, element, carry, unroll=unroll)
            for k in range(12):
                if add:
                    back[sweep, k, last, at] += carry[k]
                else:
                    back[sweep, k, last, at] = carry[k]

    def image(sweep, q):
        result = []
        for c in range(3):
            halves = []
            for x in range(2):
                k = 4 * c + 2 * x
                s, d = back[sweep, k, q], back[sweep, k + 1, q]
                halves.append((s - d) + upper(s + d))
            s, d = halves
            result.append((s - d) + right(s + d))
        return result

    def finish(q, sweep):
        moved = image(sweep, q)
        r0, r1, r2 = [right_side[c, q] - moved[c] for c in range(3)]
        if sweep == SWEEPS:
            for c, value in enumerate((r0, r1, r2)):
                resid[c, q] = value
            return sweep
        i00, i11, i22, i01, i02, i12 = [inverse[k, q] for k in range(6)]
        cur[0, q] += i00 * r0 + i01 * r1 + i02 * r2
        cur[1, q] += i01 * r0 + i11 * r1 + i12 * r2
        cur[2, q] += i02 * r0 + i12 * r1 + i22 * r2
        forward(q, sweep + 1)
        return sweep

    top = PAD + size_z
    arrived([(0, -1), (0, 1)])
    flat(0, own_pairs, stage_own)
    flat(PAD, top, forward)
    flat(PAD + 1, top - 1, invert, sum_modes(PAD))
    for sweep in range(SWEEPS + 1):
        first, last = PAD + sweep, top - 1 - sweep
        elements(sweep, first, last, False, False)
        flat(first + 1, last, finish, sweep)

    arrived([side for side in SIDES if side[0] != 0])
    stage_halo(1)
    stage_halo(-1)
    flat(1, PAD, forward)
    flat(top, planes, forward)
    flat(2, PAD + 1, invert, sum_modes(1))
    flat(top - 1, planes - 1, invert, sum_modes(top - 2))
    result = pltpu.make_async_copy(
        cur.at[:, pl.ds(PAD, size_z), pl.ds(0, size_y)], smooth, result_sem
    )
    for sweep in range(SWEEPS + 1):
        if sweep == SWEEPS:
            result.start()
        elements(sweep, 1 + sweep, PAD + sweep, False, True)
        elements(sweep, top - 1 - sweep, planes - 1 - sweep, True, False)
        flat(2 + sweep, PAD + sweep + 1, finish, sweep)
        flat(top - 1 - sweep, planes - 1 - sweep, finish, sweep)
    seg_after_z = marked[0, 0:1, :]
    seg_after_y = marked[1, 0:1, :]
    maps = []
    along_z = []
    for k in range(parts_z):
        want = slab * parts_z + k
        weights = []
        places = []
        for z in range(size_z):
            weights.append(jnp.where(seg_z[z] == want, 1.0, 0.0).astype(F32))
            places.append(0.5 * (slab * size_z + z - 4 * want - 2).astype(F32))
        last = jnp.where((seg_after_z == want.astype(F32)) & (slab < slabs - 1), 1.0, 0.0)
        weights.append(last)
        places.append(0.5 * ((slab + 1) * size_z - 4 * want - 2).astype(F32))
        along_z.append((sum(weights), sum(w * p for w, p in zip(weights, places))))
        sums = [jnp.zeros((rows, width), F32) for _ in range(3)]
        turns = [jnp.zeros((rows, width), F32) for _ in range(2)]
        for z in range(size_z + 1):
            for c in range(3):
                part = weights[z] * resid[c, PAD + z]
                sums[c] = sums[c] + part
                if c < 2:
                    turns[c] = turns[c] + places[z] * part
        maps += sums + turns

    lane = lax.broadcasted_iota(jnp.int32, (2 * parts_y, rows), 1)
    part = lax.broadcasted_iota(jnp.int32, (2 * parts_y, rows), 0)
    turned = part >= parts_y
    part = jnp.where(turned, part - parts_y, part) + sub * parts_y
    segments = jnp.full((2 * parts_y, rows), -1, jnp.int32)
    for y in range(size_y):
        segments = jnp.where(lane == y, seg_y[y], segments)
    after = jnp.broadcast_to(seg_after_y[:, :rows], segments.shape)
    hit = (lane == size_y) & (after == part.astype(F32)) & (sub < subs - 1)
    weight_y = jnp.where((segments == part) | hit, 1.0, 0.0)
    place_y = 0.5 * (lane + sub * size_y - 4 * part - 2).astype(F32)
    weight_y = weight_y * jnp.where(turned, place_y, 1.0)
    along_y = jnp.sum(weight_y, axis=1, keepdims=True)

    high, low = two_parts(jnp.concatenate(maps, axis=1))
    weight_y = weight_y.astype(BF16)
    by_y = jnp.dot(weight_y, high, preferred_element_type=F32)
    by_y = by_y + jnp.dot(weight_y, low, preferred_element_type=F32)
    tall = jnp.concatenate(
        [by_y[:, width * k : width * (k + 1)] for k in range(len(maps))], axis=0
    )
    by_x = lax.dot_general(
        jnp.concatenate(two_parts(tall), axis=1),
        weights_x[...],
        (((1,), (1,)), ((), ())),
        preferred_element_type=F32,
    )
    pick = lax.broadcasted_iota(jnp.int32, (parts_y, spread), 0) == (
        lax.broadcasted_iota(jnp.int32, (parts_y, spread), 1) // parts_x
    )

    def picked(block):
        return jnp.sum(jnp.where(pick, block, 0.0), axis=0, keepdims=True)

    def chosen(k, turn_y, turn_x):
        start = (2 * k + turn_y) * parts_y
        return picked(by_x[start : start + parts_y, turn_x * spread : (turn_x + 1) * spread])

    count_y, moment_y = picked(along_y[0:parts_y]), picked(along_y[parts_y : 2 * parts_y])
    for k in range(parts_z):
        b = 5 * k
        count_z, moment_z = along_z[k]
        centre_x, centre_y, centre_z = moment_x / count_x, moment_y / count_y, moment_z / count_z
        scale = lax.rsqrt(count_x * count_y * count_z)
        s0, s1, s2 = chosen(b, 0, 0), chosen(b + 1, 0, 0), chosen(b + 2, 0, 0)
        t0 = chosen(b + 2, 1, 0) - chosen(b + 4, 0, 0) - (centre_y * s2 - centre_z * s1)
        t1 = chosen(b + 3, 0, 0) - chosen(b + 2, 0, 1) - (centre_z * s0 - centre_x * s2)
        t2 = chosen(b + 1, 0, 1) - chosen(b, 1, 0) - (centre_x * s1 - centre_y * s0)
        for c, value in enumerate((s0, s1, s2, t0, t1, t2)):
            coarse[c, k : k + 1, :] = value * scale

    for dz, dy in SIDES:

        @pl.when(present(dz, dy))
        def _():
            for copy in copies[dz, dy]:
                copy.wait_send()

    result.wait()


def on_device(field_init, load, modulus, seg_z, seg_y, seg_x):
    size_z, size_y, width = modulus.shape
    planes = size_z + 2 * PAD
    rows = size_y + 2 * PAD
    hbm = pl.BlockSpec(memory_space=pltpu.HBM)
    vmem = pl.BlockSpec(memory_space=pltpu.VMEM)
    block = (planes, rows, width)
    corner_tiles = max((len(corner_planes(dz, size_z)) + 1) // 2 for dz in (-1, 1))
    smooth, coarse = pl.pallas_call(
        functools.partial(kernel, unroll=UNROLL),
        out_shape=(
            jax.ShapeDtypeStruct((3, size_z, size_y, width), F32),
            jax.ShapeDtypeStruct((6, size_z // 4, size_y * width // 16), F32),
        ),
        in_specs=[hbm] * 6,
        out_specs=(hbm, vmem),
        scratch_shapes=[
            pltpu.SMEM(seg_z.shape, jnp.int32),
            pltpu.SMEM(seg_y.shape, jnp.int32),
            pltpu.VMEM((1, width), jnp.int32),
            pltpu.VMEM(field_init.shape, F32),
            pltpu.VMEM(load.shape, F32),
            pltpu.VMEM(modulus.shape, F32),
            pltpu.SemaphoreType.DMA((6,)),
            pltpu.SemaphoreType.DMA,
            pltpu.VMEM((2, 7, size_z // 2, 8, width), F32),
            pltpu.VMEM((2, 7, size_z // 2, 8, width), F32),
            pltpu.VMEM((2, 2, corner_tiles, 8, width), F32),
            pltpu.VMEM((2, 2, corner_tiles, 8, width), F32),
            pltpu.VMEM((7, planes, size_y, width), F32),
            pltpu.VMEM((2, 8, width), F32),
            pltpu.VMEM((2, 8, width), F32),
            pltpu.VMEM((size_y * width // 8, 2 * width), BF16),
            pltpu.VMEM((3, *block), F32),
            pltpu.VMEM((3, *block), F32),
            pltpu.VMEM(block, F32),
            pltpu.VMEM((6, *block), F32),
            pltpu.VMEM((SWEEPS + 1, 12, *block), F32),
            pltpu.VMEM((SWEEPS + 1, 12, *block), F32),
            pltpu.VMEM((3, *block), F32),
            pltpu.SemaphoreType.DMA((len(SIDES), 4)),
            pltpu.SemaphoreType.DMA((len(SIDES), 4)),
        ],
        compiler_params=pltpu.CompilerParams(
            collective_id=0, has_side_effects=True, vmem_limit_bytes=(64 << 20) - (64 << 10)
        ),
        name="sweeps",
    )(seg_z, seg_y, seg_x.reshape(1, width), field_init, load, modulus)
    return smooth, coarse


def solution(mesh):
    in_specs = (
        P(None, "slab", "sub", None),
        P(None, "slab", "sub", None),
        P("slab", "sub", None),
        P("slab"),
        P("sub"),
        P(),
    )
    out_specs = (P(None, "slab", "sub", None), P(None, "slab", "sub"))
    return jax.shard_map(
        on_device, mesh=mesh, in_specs=in_specs, out_specs=out_specs, check_vma=False
    )
```
